128 devices in a mesh: ty: 8 (over x_hi, y), tx: 16 (over z, x_lo, core).
Axes of the slice: x: 4 (x_hi: 2, x_lo: 2; x = x_hi * 2 + x_lo), y: 4, z: 4, core: 2. Of those that a mesh axis runs over, the one named last changes fastest.
Arguments:
- region_state: bfloat16 [8, 16, 256, 1024], P('ty', 'tx'), may hold values from -6 to 6
- global_latent: bfloat16 [65536, 1024], P(('ty', 'tx')), may hold values from -6 to 6
- send_rows: int32 [128, 1024], P(('ty', 'tx')), may hold values from 0 to 511, as said below
- recv_slots: int32 [8, 16, 1024], P('ty', 'tx'), may hold values from 0 to 1023, as said below
- regrid_weight: float32 [8, 16, 256, 4], P('ty', 'tx'), may hold values from 0.2 to 1
- window_mask: int32 [8, 16, 5], P('ty', 'tx'), may hold values from 0 to 1, as said below
- norm_gain: bfloat16 [1024], replicated, may hold values from 0.25 to 1.75
- w_query: bfloat16 [1024, 1024], replicated, may hold values from -0.1875 to 0.1875
- w_key: bfloat16 [1024, 1024], replicated, may hold values from -0.1875 to 0.1875
- w_value: bfloat16 [1024, 1024], replicated, may hold values from -0.1875 to 0.1875
- w_out: bfloat16 [1024, 1024], replicated, may hold values from -0.1875 to 0.1875
- out_grad: bfloat16 [8, 16, 256, 1024], P('ty', 'tx'), may hold values from -6 to 6
Outputs:
- updated: bfloat16 [8, 16, 256, 1024], P('ty', 'tx')
- state_grad: bfloat16 [8, 16, 256, 1024], P('ty', 'tx')
- global_grad: bfloat16 [65536, 1024], P(('ty', 'tx'))
- weight_grads: float32 [4, 1024, 1024], P(None, ('ty', 'tx'))
The draws below stay inside these ranges and needn't reach their ends.
Inputs may be any that keep to these rules, and one draw needn't show every extreme that they name: `send_rows`: each device's list names each of its 512 global rows equally often. `recv_slots`: on every tile each of the 1024 received slots is read, all about equally often. `window_mask`: entry 0 is 1; a flag is 0 where the tile named lies outside the grid; two neighbouring tiles flag each other alike.
All inputs are finite; a program needn't handle non-finite values.
Results may differ from the reference program's by a relative error of at most 0.015.
Values may be sent and summed in bfloat16 or wider, within the bound.
No kernel may reach another device: no remote copies, remote signals or barrier semaphores. Data moves between devices by JAX's collectives and lax.ppermute only.
A program may use at most 128 MiB of HBM per device.

```python
import jax
import jax.numpy as jnp
from jax import lax

HEADS = 8
HEAD_SIZE = 128
D = 1024
R_DEV = 256
SOURCES = 4
CAP = 8
GLOBAL_DEV = 512
GLOBAL_ROWS = 65536
N_TY = 8
N_TX = 16


def draw_send_rows(key, part):
    key = jax.random.fold_in(key, 3)
    count = N_TY * N_TX * CAP
    base = jnp.broadcast_to(jnp.arange(count, dtype=jnp.int32), (N_TY * N_TX, count))
    mixed = jax.random.permutation(key, base, axis=-1, independent=True)
    return mixed % GLOBAL_DEV


def draw_recv_slots(key, part):
    key = jax.random.fold_in(key, 5)
    count = R_DEV * SOURCES
    base = jnp.broadcast_to(jnp.arange(count, dtype=jnp.int32), (N_TY, N_TX, count))
    mixed = jax.random.permutation(key, base, axis=-1, independent=True)
    return mixed % (N_TY * N_TX * CAP)


def draw_window_mask(key, part):
    key = jax.random.fold_in(key, 7)
    first_key, second_key = jax.random.split(key)
    row_index = jnp.arange(N_TY, dtype=jnp.int32)[:, None]
    col_index = jnp.arange(N_TX, dtype=jnp.int32)[None, :]
    vertical = (jax.random.randint(first_key, (N_TY, N_TX), 0, 4) > 0).astype(jnp.int32)
    vertical = vertical * (row_index < N_TY - 1).astype(jnp.int32)
    sideways = (jax.random.randint(second_key, (N_TY, N_TX), 0, 4) > 0).astype(jnp.int32)
    sideways = sideways * (col_index < N_TX - 1).astype(jnp.int32)
    upward = jnp.concatenate([jnp.zeros((1, N_TX), jnp.int32), vertical[:-1]], axis=0)
    leftward = jnp.concatenate([jnp.zeros((N_TY, 1), jnp.int32), sideways[:, :-1]], axis=1)
    itself = jnp.ones((N_TY, N_TX), jnp.int32)
    return jnp.stack([itself, upward, vertical, leftward, sideways], axis=-1)


def block_scale(own_key, shape, cuts, least, top_value):
    gain = 1.0
    for axis_at, parts in cuts:
        steps = jax.random.uniform(jax.random.fold_in(jax.random.fold_in(own_key, 6), axis_at), (parts,), jnp.float32, least / len(cuts), top_value / len(cuts))
        gain = gain * jnp.repeat(jnp.exp(steps), shape[axis_at] // parts).reshape((-1,) + (1,) * (len(shape) - 1 - axis_at))
    return gain


def normal_values(stream_key, dims, width, reach, cuts=(), held_as=jnp.bfloat16):
    level = block_scale(stream_key, dims, cuts, -0.22, 0.18) if cuts else 1.0
    array = jax.random.normal(stream_key, dims, jnp.float32) * width * level
    return jnp.minimum(jnp.maximum(array, -reach), reach).astype(held_as)


def setup_inputs(seed: int = 0) -> dict:
    key_list = jax.random.split(jax.random.key(seed), 13)
    return {
        "region_state": normal_values(key_list[0], (N_TY, N_TX, R_DEV, D), 1.0, 6.0, ((0, 8), (1, 16))),
        "global_latent": normal_values(key_list[1], (GLOBAL_ROWS, D), 1.0, 6.0, ((0, 128),)),
        "send_rows": draw_send_rows(jax.random.fold_in(key_list[12], 71), 0),
        "recv_slots": draw_recv_slots(jax.random.fold_in(key_list[12], 71), 0),
        "regrid_weight": jnp.clip(0.2 + 0.8 * jax.random.uniform(key_list[4], (N_TY, N_TX, R_DEV, SOURCES), jnp.float32) ** block_scale(key_list[4], (N_TY, N_TX, R_DEV, SOURCES), ((0, 8), (1, 16)), -0.2, 0.2), 0.2, 1.0),
        "window_mask": draw_window_mask(jax.random.fold_in(key_list[12], 71), 0),
        "norm_gain": jnp.clip(1.0 + 0.15 * jax.random.normal(key_list[6], (D,), jnp.float32), 0.25, 1.75).astype(jnp.bfloat16),
        "w_query": normal_values(key_list[7], (D, D), D ** -0.5, 0.1875),
        "w_key": normal_values(key_list[8], (D, D), D ** -0.5, 0.1875),
        "w_value": normal_values(key_list[9], (D, D), D ** -0.5, 0.1875),
        "w_out": normal_values(key_list[10], (D, D), D ** -0.5, 0.1875),
        "out_grad": normal_values(key_list[11], (N_TY, N_TX, R_DEV, D), 1.0, 6.0, ((0, 8), (1, 16))),
    }


EPSILON = 1e-05

def barrier_round(values):
    rounded = lax.optimization_barrier(values.astype(jnp.bfloat16))
    return rounded.astype(jnp.float32)

def five_blocks(field):
    padded = jnp.pad(field, ((1, 1), (1, 1), (0, 0), (0, 0)))
    return jnp.stack([field, padded[:-2, 1:-1], padded[2:, 1:-1], padded[1:-1, :-2], padded[1:-1, 2:]], axis=2)

def collect_blocks(pieces):
    padded = jnp.pad(pieces, ((1, 1), (1, 1), (0, 0), (0, 0), (0, 0)))
    total = pieces[:, :, 0] + padded[2:, 1:-1, 1] + padded[:-2, 1:-1, 2]
    return total + padded[1:-1, 2:, 3] + padded[1:-1, :-2, 4]

def device_attention(query_rows, key_blocks, value_blocks, flags, grad_rows):
    num_rows = query_rows.shape[0]
    attn_scale = HEAD_SIZE ** (-0.5)
    query_heads = query_rows.astype(jnp.float32).reshape(num_rows, HEADS, HEAD_SIZE)
    key_heads = key_blocks.astype(jnp.float32).reshape(5 * num_rows, HEADS, HEAD_SIZE)
    value_heads = value_blocks.astype(jnp.float32).reshape(5 * num_rows, HEADS, HEAD_SIZE)
    grad_heads = grad_rows.astype(jnp.float32).reshape(num_rows, HEADS, HEAD_SIZE)
    valid = jnp.repeat(flags > 0, num_rows)
    scores = jnp.where(valid, jnp.einsum('qhd,khd->hqk', query_heads, key_heads) * attn_scale, -jnp.inf)
    highest = lax.optimization_barrier(jnp.max(scores, axis=-1, keepdims=True))
    log_total = highest + jnp.log(lax.optimization_barrier(jnp.sum(jnp.exp(scores - highest), axis=-1, keepdims=True)))
    prob_exact = jnp.exp(scores - log_total)
    prob_weights = barrier_round(prob_exact)
    attended = jnp.einsum('hqk,khd->qhd', prob_weights, value_heads).reshape(num_rows, -1).astype(jnp.bfloat16)
    attended_heads = attended.astype(jnp.float32).reshape(num_rows, HEADS, HEAD_SIZE)
    row_delta = jnp.einsum('qhd,qhd->hq', grad_heads, attended_heads)[:, :, None]
    grad_prob = jnp.einsum('qhd,khd->hqk', grad_heads, value_heads)
    dscore = barrier_round(prob_exact * (grad_prob - row_delta) * attn_scale)
    grad_query = jnp.einsum('hqk,khd->qhd', dscore, key_heads).reshape(num_rows, -1).astype(jnp.bfloat16)
    key_parts = jnp.einsum('hqk,qhd->khd', dscore, query_heads).reshape(5, num_rows, -1)
    value_parts = jnp.einsum('hqk,qhd->khd', prob_weights, grad_heads).reshape(5, num_rows, -1)
    return (attended, grad_query, key_parts, value_parts)

def reference(region_state, global_latent, send_rows, recv_slots, regrid_weight, window_mask, norm_gain, w_query, w_key, w_value, w_out, out_grad):
    n_dev = N_TY * N_TX
    slot_total = n_dev * CAP
    model_width = region_state.shape[3]
    full_shape = region_state.shape
    slot_ids = recv_slots.reshape(n_dev, -1)
    owner = jnp.arange(n_dev, dtype=jnp.int32)[:, None]
    sender = slot_ids // CAP
    local_rows = send_rows[sender, owner * CAP + slot_ids % CAP]
    source_rows = sender * GLOBAL_DEV + local_rows
    pulled = global_latent[source_rows].astype(jnp.float32).reshape(N_TY, N_TX, R_DEV, SOURCES, model_width)
    forcing = lax.optimization_barrier(jnp.sum(regrid_weight[..., None] * pulled, axis=3))
    pre_norm = region_state.astype(jnp.float32) + forcing
    inverse = lax.rsqrt(lax.optimization_barrier(jnp.mean(pre_norm * pre_norm, axis=-1, keepdims=True)) + EPSILON)
    normed = pre_norm * inverse
    normed_in = (normed * norm_gain.astype(jnp.float32)).astype(jnp.bfloat16)
    flat_in = normed_in.reshape(-1, model_width)

    def project(matrix):
        return jnp.dot(flat_in, matrix, preferred_element_type=jnp.float32).astype(jnp.bfloat16).reshape(full_shape)
    queries = project(w_query)
    key_field = project(w_key)
    value_field = project(w_value)
    grad_attended = jnp.dot(out_grad.reshape(-1, model_width), w_out.T, preferred_element_type=jnp.float32)
    grad_attended = grad_attended.astype(jnp.bfloat16).reshape(full_shape)
    key_near = five_blocks(key_field)
    value_near = five_blocks(value_field)

    def per_band(items):
        return jax.vmap(device_attention)(*items)
    attended, grad_query, key_parts, value_parts = lax.map(per_band, (queries, key_near, value_near, window_mask, grad_attended))
    grad_key = collect_blocks(key_parts).astype(jnp.bfloat16)
    grad_value = collect_blocks(value_parts).astype(jnp.bfloat16)
    output_term = jnp.dot(attended.reshape(-1, model_width), w_out, preferred_element_type=jnp.float32).reshape(full_shape)
    updated = (region_state.astype(jnp.float32) + output_term).astype(jnp.bfloat16)

    def backward(grad_field, matrix):
        return jnp.dot(grad_field.reshape(-1, model_width), matrix.T, preferred_element_type=jnp.float32)
    grad_normed_in = backward(grad_query, w_query) + backward(grad_key, w_key) + backward(grad_value, w_value)

    def outer(left_field, right_field):
        return jnp.dot(left_field.reshape(-1, model_width).T, right_field.reshape(-1, model_width), preferred_element_type=jnp.float32)
    weight_grads = jnp.stack([outer(normed_in, grad_query), outer(normed_in, grad_key), outer(normed_in, grad_value), outer(attended, out_grad)])
    grad_normed = grad_normed_in.reshape(full_shape) * norm_gain.astype(jnp.float32)
    grad_pre = inverse * (grad_normed - normed * lax.optimization_barrier(jnp.mean(grad_normed * normed, axis=-1, keepdims=True)))
    state_grad = (out_grad.astype(jnp.float32) + grad_pre).astype(jnp.bfloat16)
    use_grad = regrid_weight[..., None] * grad_pre[:, :, :, None, :]
    slot_grad = jnp.zeros((n_dev, slot_total, model_width), jnp.float32).at[owner, slot_ids].add(use_grad.reshape(n_dev, -1, model_width))
    slot_sent = barrier_round(slot_grad)
    every_slot = jnp.arange(slot_total, dtype=jnp.int32)[None, :]
    slot_sender = every_slot // CAP
    slot_rows = slot_sender * GLOBAL_DEV + send_rows[slot_sender, owner * CAP + every_slot % CAP]
    global_grad = jnp.zeros((n_dev * GLOBAL_DEV, model_width), jnp.float32).at[slot_rows.reshape(-1)].add(slot_sent.reshape(-1, model_width))
    return (updated, state_grad, global_grad.astype(jnp.bfloat16), weight_grads)
```

```python
import functools
import jax
import jax.numpy as jnp
from jax import lax
from jax.experimental import pallas as pl
from jax.experimental.pallas import tpu as pltpu
from jax.sharding import PartitionSpec as P

HEADS = 8
HEAD_SIZE = 128
EPSILON = 1e-05
LOG2_E = 1.4426950408889634
BF16 = jnp.bfloat16
F32 = jnp.float32
NN = (((1,), (0,)), ((), ()))
NT = (((1,), (1,)), ((), ()))
TN = (((0,), (0,)), ((), ()))


def mm(left, right, dims=NN):
    return lax.dot_general(left, right, dims, preferred_element_type=F32)


def params(**more):
    return pltpu.CompilerParams(vmem_limit_bytes=56 * 1024 * 1024, **more)


def pick_kernel(rows_ref, table_ref, out_ref):
    table_rows = table_ref.shape[0]
    hit = lax.broadcasted_iota(jnp.int32, (table_rows, rows_ref.shape[1]), 0) == rows_ref[...]
    out_ref[...] = mm(hit.astype(F32).astype(BF16), table_ref[...], TN).astype(BF16)


def pick_rows(rows, table):
    count, width, step = rows.shape[1], table.shape[1], 256
    return pl.pallas_call(
        pick_kernel,
        grid=(count // step,),
        in_specs=[
            pl.BlockSpec((1, step), lambda i: (0, i)),
            pl.BlockSpec(table.shape, lambda i: (0, 0)),
        ],
        out_specs=pl.BlockSpec((step, width), lambda i: (i, 0)),
        out_shape=jax.ShapeDtypeStruct((count, width), BF16),
        compiler_params=params(),
        name="pick_rows",
    )(rows, table)


def add_kernel(rows_ref, sent_ref, out_ref):
    step = out_ref.shape[0]
    ids = lax.broadcasted_iota(jnp.int32, (step, rows_ref.shape[1]), 0) + pl.program_id(0) * step
    hit = (ids == rows_ref[...]).astype(F32).astype(BF16)
    out_ref[...] = mm(hit, sent_ref[...]).astype(BF16)


def add_rows(rows, sent, table_rows):
    step = 256
    return pl.pallas_call(
        add_kernel,
        grid=(table_rows // step,),
        in_specs=[
            pl.BlockSpec(rows.shape, lambda i: (0, 0)),
            pl.BlockSpec(sent.shape, lambda i: (0, 0)),
        ],
        out_specs=pl.BlockSpec((step, sent.shape[1]), lambda i: (i, 0)),
        out_shape=jax.ShapeDtypeStruct((table_rows, sent.shape[1]), BF16),
        compiler_params=params(),
        name="add_rows",
    )(rows, sent)


def blend_kernel(slots_ref, blend_ref, incoming_ref, state_ref, gain_ref, in_ref, normed_ref, inverse_ref, high_ref, low_ref):
    rows, slots = blend_ref.shape[0], incoming_ref.shape[0]
    lanes = lax.broadcasted_iota(jnp.int32, (rows, slots), 1)
    spread = jnp.zeros((rows, slots), F32)
    for k in range(blend_ref.shape[1]):
        spread = spread + jnp.where(lanes == slots_ref[:, k : k + 1], blend_ref[:, k : k + 1], 0.0)
    high = spread.astype(BF16)
    low = (spread - high.astype(F32)).astype(BF16)
    high_ref[...] = high
    low_ref[...] = low
    incoming = incoming_ref[...]
    pre = state_ref[...].astype(F32) + (mm(high, incoming) + mm(low, incoming))
    inverse = lax.rsqrt(jnp.mean(pre * pre, axis=-1, keepdims=True) + EPSILON)
    normed = pre * inverse
    normed_ref[...] = normed
    inverse_ref[...] = jnp.broadcast_to(inverse, inverse_ref.shape)
    in_ref[...] = (normed * gain_ref[...].astype(F32)).astype(BF16)


def blend_norm(slots, blend, incoming, state, gain):
    rows, width = state.shape
    spread = jax.ShapeDtypeStruct((rows, incoming.shape[0]), BF16)
    return pl.pallas_call(
        blend_kernel,
        out_shape=(
            jax.ShapeDtypeStruct((rows, width), BF16),
            jax.ShapeDtypeStruct((rows, width), F32),
            jax.ShapeDtypeStruct((rows, 128), F32),
            spread,
            spread,
        ),
        compiler_params=params(),
        name="blend_norm",
    )(slots, blend, incoming, state, gain)


def attend_kernel(
    chunk, mask_ref, own_ref, up_ref, down_ref, left_ref, right_ref, state_ref, grad_ref, wq_ref, wk_ref, wv_ref, wo_ref,
    updated_ref, own_grad_ref, near_grad_ref, qkv_ref, out_ref,
    x_all, x_turned, grads, total,
):
    head = pl.program_id(0)
    rows = own_ref.shape[0]
    blocks = x_all.shape[0] // rows

    @pl.when(head == 0)
    def _():
        for b, ref in enumerate((own_ref, up_ref, down_ref, left_ref, right_ref)):
            x_all[b * rows : (b + 1) * rows] = ref[...]
            x_turned[:, b * rows : (b + 1) * rows] = ref[...].T
        grads[...] = jnp.zeros_like(grads)
        total[...] = jnp.zeros_like(total)

    w_both = jnp.concatenate([wk_ref[...], wv_ref[...]], axis=1)
    grad_out = grad_ref[...]
    query_t = mm(wq_ref[...], own_ref[...], (((0,), (1,)), ((), ()))).astype(BF16)
    query = query_t.astype(F32).T.astype(BF16)
    g_t = mm(wo_ref[...], grad_out, NT).astype(BF16)
    g = g_t.astype(F32).T.astype(BF16)
    both = mm(x_all[...], w_both).astype(BF16)
    key, value = both[:, :HEAD_SIZE], both[:, HEAD_SIZE:]
    scale = HEAD_SIZE ** (-0.5)
    raw = mm(key, query_t)
    scores = jnp.concatenate(
        [
            raw[b * rows : (b + 1) * rows] * (scale * LOG2_E) + jnp.where(mask_ref[0, b] > 0, 0.0, -1e30)
            for b in range(blocks)
        ],
        axis=0,
    )
    highest = jnp.max(scores, axis=0, keepdims=True)
    raised = jnp.exp2(scores - highest)
    prob = raised * (1.0 / jnp.sum(raised, axis=0, keepdims=True))
    weights = prob.astype(BF16)
    attended_t = mm(value, weights, TN).astype(BF16)
    delta = jnp.sum(g_t.astype(F32) * attended_t.astype(F32), axis=0, keepdims=True)
    dscore = (prob * (mm(value, g_t) - delta) * scale).astype(BF16)
    dquery_t = mm(key, dscore, TN).astype(BF16)
    dquery = dquery_t.astype(F32).T.astype(BF16)
    dboth = jnp.concatenate([mm(dscore, query), mm(weights, g)], axis=1).astype(BF16)
    total[...] += mm(attended_t.astype(F32).T.astype(BF16), wo_ref[...])
    grads[...] += mm(dboth, w_both, NT)
    grads[:rows] += mm(dquery, wq_ref[...], NT)
    width = grad_out.shape[1]
    split = (-1, 2, chunk, HEAD_SIZE)
    dwq = mm(x_turned[:, :rows], dquery).reshape(split)
    dwb = mm(x_turned[...], dboth)
    dwk = dwb[:, :HEAD_SIZE].reshape(split)
    dwv = dwb[:, HEAD_SIZE:].reshape(split)
    dwo = mm(attended_t, grad_out).reshape(-1, 2, chunk, width)
    for c in range(2):
        for m, part in enumerate((dwq, dwk, dwv)):
            qkv_ref[c, m] = part[:, c].reshape(width // 2, HEAD_SIZE).astype(BF16)
        out_ref[c] = dwo[:, c].reshape(HEAD_SIZE // 2, width).astype(BF16)

    @pl.when(head == pl.num_programs(0) - 1)
    def _():
        updated_ref[...] = (state_ref[...].astype(F32) + total[...]).astype(BF16)
        own_grad_ref[...] = grads[:rows]
        near_grad_ref[...] = grads[rows:].reshape(near_grad_ref.shape).astype(BF16)


def attend(mask, tiles, state, grad_out, w_query, w_key, w_value, w_out, chunk):
    rows, width = state.shape
    near = len(tiles)
    whole = lambda: pl.BlockSpec((rows, width), lambda h: (0, 0))
    columns = lambda: pl.BlockSpec((width, HEAD_SIZE), lambda h: (0, h))
    return pl.pallas_call(
        functools.partial(attend_kernel, chunk),
        grid=(HEADS,),
        in_specs=[pl.BlockSpec(memory_space=pltpu.SMEM)]
        + [whole() for _ in range(near + 2)]
        + [columns(), columns(), columns(), pl.BlockSpec((HEAD_SIZE, width), lambda h: (h, 0))],
        out_specs=[
            whole(),
            whole(),
            pl.BlockSpec((near - 1, rows, width), lambda h: (0, 0, 0)),
            pl.BlockSpec((2, 3, width // 2, HEAD_SIZE), lambda h: (0, 0, 0, h)),
            pl.BlockSpec((2, HEAD_SIZE // 2, width), lambda h: (0, h, 0)),
        ],
        out_shape=(
            jax.ShapeDtypeStruct((rows, width), BF16),
            jax.ShapeDtypeStruct((rows, width), F32),
            jax.ShapeDtypeStruct((near - 1, rows, width), BF16),
            jax.ShapeDtypeStruct((2, 3, width // 2, width), BF16),
            jax.ShapeDtypeStruct((2, width // 2, width), BF16),
        ),
        scratch_shapes=[
            pltpu.VMEM((near * rows, width), BF16),
            pltpu.VMEM((width, near * rows), BF16),
            pltpu.VMEM((near * rows, width), F32),
            pltpu.VMEM((rows, width), F32),
        ],
        compiler_params=params(),
        name="attend",
    )(mask, *tiles, state, grad_out, w_query, w_key, w_value, w_out)


def finish_kernel(own_ref, up_ref, down_ref, left_ref, right_ref, normed_ref, inverse_ref, gain_ref, grad_ref, high_ref, low_ref, state_grad_ref, slot_ref):
    total = own_ref[...]
    for ref in (up_ref, down_ref, left_ref, right_ref):
        total = total + ref[...].astype(F32)
    grad = total * gain_ref[...].astype(F32)
    normed = normed_ref[...]
    grad = inverse_ref[:, :1] * (grad - normed * jnp.mean(grad * normed, axis=-1, keepdims=True))
    state_grad_ref[...] = (grad_ref[...].astype(F32) + grad).astype(BF16)
    top = grad.astype(BF16)
    rest = (grad - top.astype(F32)).astype(BF16)
    slot_ref[...] = (mm(high_ref[...], top, TN) + (mm(high_ref[...], rest, TN) + mm(low_ref[...], top, TN))).astype(BF16)


def finish(own, near, normed, inverse, gain, grad_out, high, low):
    rows, width = own.shape
    return pl.pallas_call(
        finish_kernel,
        out_shape=(
            jax.ShapeDtypeStruct((rows, width), BF16),
            jax.ShapeDtypeStruct((high.shape[1], width), BF16),
        ),
        compiler_params=params(),
        name="finish",
    )(own, *near, normed, inverse, gain, grad_out, high, low)


def exchange(chunks, axis):
    count = chunks.shape[0]
    here = lax.axis_index(axis)
    arrived = [
        lax.ppermute(
            lax.dynamic_index_in_dim(chunks, (here + step) % count, 0, keepdims=False),
            axis,
            [(i, (i + step) % count) for i in range(count)],
        )
        for step in range(1, count)
    ]
    total = lax.dynamic_index_in_dim(chunks, here, 0, keepdims=False).astype(F32)
    for piece in arrived:
        total = total + piece.astype(F32)
    return total


def passed_along(block, axis, distance):
    count = lax.axis_size(axis)
    route = [(i, i + distance) for i in range(count) if 0 <= i + distance < count]
    return lax.ppermute(block, axis, route)


TY = ("x_hi", "y")
TX = ("z", "x_lo", "core")
X = ("x_hi", "x_lo")


def reduce_weights(qkv, out):
    width = qkv.shape[-1]
    whole = jnp.concatenate([qkv, out[:, None]], axis=1)
    total = exchange(whole, "core").astype(BF16)
    sizes = [lax.axis_size(a) for a in ("x_hi", "y", "z", "x_lo")]
    chunk = total.shape[1] // (sizes[0] * sizes[1] * sizes[2] * sizes[3])
    total = total.reshape(4, *sizes, chunk, width)
    total = exchange(jnp.moveaxis(total, 3, 0), "z").astype(BF16)
    total = exchange(jnp.moveaxis(total, 2, 0), "y").astype(BF16)
    total = jnp.transpose(total, (1, 2, 0, 3, 4)).reshape(sizes[0] * sizes[3], 4, chunk, width)
    return exchange(total, X)


def body(
    region_state,
    global_latent,
    send_rows,
    recv_slots,
    regrid_weight,
    window_mask,
    norm_gain,
    w_query,
    w_key,
    w_value,
    w_out,
    out_grad,
):
    state, grad_out = region_state[0, 0], out_grad[0, 0]
    rows, width = state.shape
    gain = norm_gain[None]
    devices = lax.axis_size(TY + TX)
    outgoing = pick_rows(send_rows, global_latent)
    incoming = lax.all_to_all(outgoing, TY + TX, split_axis=0, concat_axis=0, tiled=True)
    normed_in, normed, inverse, high, low = blend_norm(
        recv_slots.reshape(rows, -1), regrid_weight[0, 0], incoming, state, gain
    )
    tiles = (
        normed_in,
        passed_along(normed_in, TY, 1),
        passed_along(normed_in, TY, -1),
        passed_along(normed_in, TX, 1),
        passed_along(normed_in, TX, -1),
    )
    updated, own, near, qkv, out = attend(
        window_mask[0], tiles, state, grad_out, w_query, w_key, w_value, w_out, width // devices
    )
    weight_grads = reduce_weights(qkv, out)
    returned = (
        passed_along(near[0], TY, -1),
        passed_along(near[1], TY, 1),
        passed_along(near[2], TX, -1),
        passed_along(near[3], TX, 1),
    )
    state_grad, slots = finish(own, returned, normed, inverse, gain, grad_out, high, low)
    sent_back = lax.all_to_all(slots, TY + TX, split_axis=0, concat_axis=0, tiled=True)
    global_grad = add_rows(send_rows, sent_back, global_latent.shape[0])
    return (updated[None, None], state_grad[None, None], global_grad, weight_grads)


def solution(mesh):
    ty, tx = mesh.devices.shape
    y, z = max(ty // 2, 1), tx // 4
    fine = jax.sharding.Mesh(mesh.devices.reshape(ty // y, y, z, 2, 2), TY + TX)
    tiles = P(TY, TX)
    flat = P(TY + TX)
    return jax.shard_map(
        body,
        mesh=fine,
        in_specs=(tiles, flat, flat, tiles, tiles, tiles, P(), P(), P(), P(), P(), tiles),
        out_specs=(tiles, tiles, flat, P(None, TY + TX)),
        check_vma=False,
    )
```

```python
import functools
import jax
import jax.numpy as jnp
from jax import lax
from jax.experimental import pallas as pl
from jax.experimental.pallas import tpu as pltpu
from jax.sharding import PartitionSpec as P

HEADS = 8
HEAD_SIZE = 128
EPSILON = 1e-05
LOG2_E = 1.4426950408889634
BF16 = jnp.bfloat16
F32 = jnp.float32
NN = (((1,), (0,)), ((), ()))
NT = (((1,), (1,)), ((), ()))
TN = (((0,), (0,)), ((), ()))


def mm(left, right, dims=NN):
    return lax.dot_general(left, right, dims, preferred_element_type=F32)


def params(mib):
    return pltpu.CompilerParams(vmem_limit_bytes=mib * 1024 * 1024)


def pick_kernel(rows_ref, table_ref, out_ref):
    table_rows = table_ref.shape[0]
    hit = lax.broadcasted_iota(jnp.int32, (table_rows, rows_ref.shape[1]), 0) == rows_ref[...]
    out_ref[...] = mm(hit.astype(F32).astype(BF16), table_ref[...], TN).astype(BF16)


def pick_rows(rows, table):
    count, width, step = rows.shape[1], table.shape[1], 256
    return pl.pallas_call(
        pick_kernel,
        grid=(count // step,),
        in_specs=[
            pl.BlockSpec((1, step), lambda i: (0, i)),
            pl.BlockSpec(table.shape, lambda i: (0, 0)),
        ],
        out_specs=pl.BlockSpec((step, width), lambda i: (i, 0)),
        out_shape=jax.ShapeDtypeStruct((count, width), BF16),
        compiler_params=params(12),
        name="pick_rows",
    )(rows, table)


def add_kernel(rows_ref, sent_ref, out_ref):
    step = out_ref.shape[0]
    ids = lax.broadcasted_iota(jnp.int32, (step, rows_ref.shape[1]), 0) + pl.program_id(0) * step
    hit = (ids == rows_ref[...]).astype(F32).astype(BF16)
    out_ref[...] = mm(hit, sent_ref[...]).astype(BF16)


def add_rows(rows, sent, table_rows):
    step = 256
    return pl.pallas_call(
        add_kernel,
        grid=(table_rows // step,),
        in_specs=[
            pl.BlockSpec(rows.shape, lambda i: (0, 0)),
            pl.BlockSpec(sent.shape, lambda i: (0, 0)),
        ],
        out_specs=pl.BlockSpec((step, sent.shape[1]), lambda i: (i, 0)),
        out_shape=jax.ShapeDtypeStruct((table_rows, sent.shape[1]), BF16),
        compiler_params=params(14),
        name="add_rows",
    )(rows, sent)


def blend_kernel(slots_ref, blend_ref, incoming_ref, state_ref, gain_ref, in_ref, normed_ref, inverse_ref, high_ref, low_ref):
    rows, slots = blend_ref.shape[0], incoming_ref.shape[0]
    lanes = lax.broadcasted_iota(jnp.int32, (rows, slots), 1)
    spread = jnp.zeros((rows, slots), F32)
    for k in range(blend_ref.shape[1]):
        spread = spread + jnp.where(lanes == slots_ref[:, k : k + 1], blend_ref[:, k : k + 1], 0.0)
    high = spread.astype(BF16)
    low = (spread - high.astype(F32)).astype(BF16)
    high_ref[...] = high
    low_ref[...] = low
    incoming = incoming_ref[...]
    pre = state_ref[...].astype(F32) + (mm(high, incoming) + mm(low, incoming))
    inverse = lax.rsqrt(jnp.mean(pre * pre, axis=-1, keepdims=True) + EPSILON)
    normed = pre * inverse
    normed_ref[...] = normed
    inverse_ref[...] = jnp.broadcast_to(inverse, inverse_ref.shape)
    in_ref[...] = (normed * gain_ref[...].astype(F32)).astype(BF16)


def blend_norm(slots, blend, incoming, state, gain):
    rows, width = state.shape
    spread = jax.ShapeDtypeStruct((rows, incoming.shape[0]), BF16)
    return pl.pallas_call(
        blend_kernel,
        out_shape=(
            jax.ShapeDtypeStruct((rows, width), BF16),
            jax.ShapeDtypeStruct((rows, width), F32),
            jax.ShapeDtypeStruct((rows, 128), F32),
            spread,
            spread,
        ),
        compiler_params=params(14),
        name="blend_norm",
    )(slots, blend, incoming, state, gain)


def attend_kernel(
    core_ref, mask_ref, own_ref, up_ref, down_ref, left_ref, right_ref, grad_ref, wq_ref, wk_ref, wv_ref, wo_ref,
    keep_ref, send_ref, attended_ref, dquery_ref, dkey_ref, dvalue_ref, x_all, x_turned,
):
    step = pl.program_id(0)
    rows = own_ref.shape[0]
    blocks = x_all.shape[0] // rows
    zs, _, _, piece, lanes = keep_ref.shape

    @pl.when(step == 0)
    def _():
        for b, ref in enumerate((own_ref, up_ref, down_ref, left_ref, right_ref)):
            x_all[b * rows : (b + 1) * rows] = ref[...]
            x_turned[:, b * rows : (b + 1) * rows] = ref[...].T

    grad_out = grad_ref[...]
    width = grad_out.shape[1]
    scale = HEAD_SIZE ** (-0.5)
    query = mm(own_ref[...], wq_ref[...]).astype(BF16)
    g = mm(grad_out, wo_ref[...]).astype(BF16)
    key = mm(x_all[...], wk_ref[...]).astype(BF16)
    value = mm(x_all[...], wv_ref[...]).astype(BF16)
    query_t, g_t = query.T, g.T
    attended_t, dquery_t, dkey, dvalue = [], [], [], []
    for h in range(lanes // HEAD_SIZE):
        at = slice(h * HEAD_SIZE, (h + 1) * HEAD_SIZE)
        raw = mm(key[:, at], query_t[at])
        scores = jnp.concatenate(
            [
                raw[b * rows : (b + 1) * rows] * (scale * LOG2_E) + jnp.where(mask_ref[0, b] > 0, 0.0, -1e30)
                for b in range(blocks)
            ],
            axis=0,
        )
        highest = jnp.max(scores, axis=0, keepdims=True)
        raised = jnp.exp2(scores - highest)
        prob = raised * (1.0 / jnp.sum(raised, axis=0, keepdims=True))
        weights = prob.astype(BF16)
        att = mm(value[:, at], weights, TN).astype(BF16)
        delta = jnp.sum(g_t[at].astype(F32) * att.astype(F32), axis=0, keepdims=True)
        dscore = (prob * (mm(value[:, at], g_t[at]) - delta) * scale).astype(BF16)
        attended_t.append(att)
        dquery_t.append(mm(key[:, at], dscore, TN).astype(BF16))
        dkey.append(mm(dscore, query[:, at]).astype(BF16))
        dvalue.append(mm(weights, g[:, at]).astype(BF16))
    attended_t = jnp.concatenate(attended_t, axis=0)
    dquery = jnp.concatenate(dquery_t, axis=0).T
    dkey = jnp.concatenate(dkey, axis=1)
    dvalue = jnp.concatenate(dvalue, axis=1)
    attended_ref[...] = attended_t.T
    dquery_ref[...] = dquery
    dkey_ref[...] = dkey
    dvalue_ref[...] = dvalue
    first = core_ref[0] == 0

    def place(z, m, where, halves):
        low, high = (half.reshape(-1, lanes) for half in halves)
        keep_ref[z, m, 0, where] = jnp.where(first, low, high).astype(BF16)
        send_ref[z, m, 0, where] = jnp.where(first, high, low).astype(BF16)

    chunk = piece // 16
    grads = (
        mm(x_turned[:, :rows], dquery),
        mm(x_turned[...], dkey),
        mm(x_turned[...], dvalue),
    )
    for m, part in enumerate(grads):
        part = part.reshape(8, zs, 2, 2, chunk, lanes)
        for z in range(zs):
            place(z, m, slice(None), [part[:, z, :, c] for c in range(2)])
    part = mm(attended_t, grad_out).reshape(2, zs, 2, 2, chunk, width)
    for z in range(zs):
        for q in range(4):
            columns = slice(q * lanes, (q + 1) * lanes)
            place(z, 3, slice(q * piece // 4, (q + 1) * piece // 4), [part[:, z, :, c, :, columns] for c in range(2)])


def attend(half, core, mask, tiles, grad_out, w_query, w_key, w_value, w_out, zs):
    rows, width = grad_out.shape
    near, lanes = len(tiles), 2 * HEAD_SIZE
    steps = width // 2 // lanes
    piece = width // 2 // zs
    whole = lambda: pl.BlockSpec((rows, width), lambda h: (0, 0), pipeline_mode=pl.Buffered(1))
    columns = lambda: pl.BlockSpec((width, lanes), lambda h: (0, half * steps + h))
    flags = lambda: pl.BlockSpec(memory_space=pltpu.SMEM)
    parts = lambda: pl.BlockSpec((zs, 4, 1, piece, lanes), lambda h: (0, 0, h, 0, 0))
    out = lambda n: pl.BlockSpec((n, lanes), lambda h: (0, h))
    part = jax.ShapeDtypeStruct((zs, 4, steps, piece, lanes), BF16)
    small = jax.ShapeDtypeStruct((rows, width // 2), BF16)
    large = jax.ShapeDtypeStruct((near * rows, width // 2), BF16)
    return pl.pallas_call(
        attend_kernel,
        grid=(steps,),
        in_specs=[flags(), flags()]
        + [whole() for _ in range(near + 1)]
        + [columns() for _ in range(4)],
        out_specs=[parts(), parts(), out(rows), out(rows), out(near * rows), out(near * rows)],
        out_shape=(part, part, small, small, large, large),
        scratch_shapes=[
            pltpu.VMEM((near * rows, width), BF16),
            pltpu.VMEM((width, near * rows), BF16),
        ],
        compiler_params=params(34),
        cost_estimate=pl.CostEstimate(flops=14 * 10**9, bytes_accessed=16 * 10**6, transcendentals=10**6),
        name="attend",
    )(core, mask, *tiles, grad_out, w_query, w_key, w_value, w_out)


def spread_kernel(dq0_ref, dq1_ref, dk0_ref, dk1_ref, dv0_ref, dv1_ref, wq_ref, wk_ref, wv_ref, up_ref, down_ref, left_ref, right_ref, own_ref):
    block = pl.program_id(0)
    half = dk0_ref.shape[1]

    def back(first, second, weight):
        return mm(first[...], weight[:half]) + mm(second[...], weight[half:])

    total = back(dk0_ref, dk1_ref, wk_ref) + back(dv0_ref, dv1_ref, wv_ref)
    for b, ref in enumerate((up_ref, down_ref, left_ref, right_ref)):

        @pl.when(block == b)
        def _():
            ref[...] = total.astype(BF16)

    @pl.when(block == pl.num_programs(0) - 1)
    def _():
        own_ref[...] = total + back(dq0_ref, dq1_ref, wq_ref)


def spread(dquery, dkey, dvalue, w_query, w_key, w_value):
    rows, half = dquery[0].shape
    width = w_query.shape[0]
    near = dkey[0].shape[0] // rows
    block = lambda: pl.BlockSpec((rows, half), lambda i: ((i + 1) % near, 0))
    small = lambda: pl.BlockSpec((rows, half), lambda i: (0, 0))
    whole = lambda n: pl.BlockSpec((n, width), lambda i: (0, 0), pipeline_mode=pl.Buffered(1))
    return pl.pallas_call(
        spread_kernel,
        grid=(near,),
        in_specs=[small(), small(), block(), block(), block(), block(), whole(width), whole(width), whole(width)],
        out_specs=[whole(rows) for _ in range(near)],
        out_shape=tuple(jax.ShapeDtypeStruct((rows, width), BF16) for _ in range(near - 1))
        + (jax.ShapeDtypeStruct((rows, width), F32),),
        compiler_params=params(20),
        cost_estimate=pl.CostEstimate(flops=6 * 10**9, bytes_accessed=14 * 10**6, transcendentals=0),
        name="spread",
    )(*dquery, *dkey, *dvalue, w_query, w_key, w_value)


def split_kernel(here_ref, keep_ref, came_ref, *out_refs):
    count = len(out_refs)
    for step, ref in enumerate(out_refs):
        at = (here_ref[0] + step) % count
        ref[...] = (keep_ref[at].astype(F32) + came_ref[at].astype(F32)).astype(BF16)


def split_sum(here, keep, came):
    count, mats, *rest = keep.shape
    whole = lambda: pl.BlockSpec((count, 1, *rest), lambda m: (0, m) + (0,) * len(rest))
    return pl.pallas_call(
        split_kernel,
        grid=(mats,),
        in_specs=[pl.BlockSpec(memory_space=pltpu.SMEM), whole(), whole()],
        out_specs=[pl.BlockSpec((1, *rest), lambda m: (m,) + (0,) * len(rest)) for _ in range(count)],
        out_shape=tuple(jax.ShapeDtypeStruct((mats, *rest), BF16) for _ in range(count)),
        compiler_params=params(10),
        cost_estimate=pl.CostEstimate(flops=10**6, bytes_accessed=6 * 10**6, transcendentals=0),
        name="split_sum",
    )(here, keep, came)


def join_kernel(pieces, here_ref, *refs):
    in_refs, out_refs, table = refs[: 2 * pieces], refs[2 * pieces : -1], refs[-1]
    ys = len(out_refs)
    _, steps, piece, lanes = in_refs[0].shape
    chunk = out_refs[0].shape[3]

    def totals():
        for half in range(2):
            group = in_refs[half * pieces : (half + 1) * pieces]
            for s in range(steps):
                total = group[0][0, s].astype(F32)
                for ref in group[1:]:
                    total = total + ref[0, s].astype(F32)
                yield half, s, total

    @pl.when(pl.program_id(0) < 3)
    def _():
        for half, s, total in totals():
            total = total.reshape(2, ys, 2, chunk, lanes)
            for y in range(ys):
                table[y, :, :, :, (half * steps + s) * lanes : (half * steps + s + 1) * lanes] = total[:, y]

    @pl.when(pl.program_id(0) == 3)
    def _():
        for half, s, total in totals():
            total = total.reshape(4, 2, 2, chunk, lanes)
            for q in range(4):
                for y in range(2):
                    table[s * 2 + y, half, :, :, q * lanes : (q + 1) * lanes] = total[q, y]

    for step, ref in enumerate(out_refs):
        ref[:, :, 0] = table[(here_ref[0] + step) % ys].astype(BF16)


def join_sum(here, first, second, ys, chunk, width):
    _, *rest = first[0].shape
    return pl.pallas_call(
        functools.partial(join_kernel, len(first)),
        grid=(4,),
        in_specs=[pl.BlockSpec(memory_space=pltpu.SMEM)]
        + [pl.BlockSpec((1, *rest), lambda m: (m, 0, 0, 0)) for _ in range(2 * len(first))],
        out_specs=[pl.BlockSpec((2, 2, 1, chunk, width), lambda m: (0, 0, m, 0, 0)) for _ in range(ys)],
        out_shape=tuple(jax.ShapeDtypeStruct((2, 2, 4, chunk, width), BF16) for _ in range(ys)),
        scratch_shapes=[pltpu.VMEM((ys, 2, 2, chunk, width), F32)],
        compiler_params=params(10),
        cost_estimate=pl.CostEstimate(flops=10**6, bytes_accessed=6 * 10**6, transcendentals=0),
        name="join_sum",
    )(here, *first, *second)


def finish_kernel(own_ref, up_ref, down_ref, left_ref, right_ref, normed_ref, inverse_ref, gain_ref, grad_ref, high_ref, low_ref, state_grad_ref, slot_ref):
    total = own_ref[...]
    for ref in (up_ref, down_ref, left_ref, right_ref):
        total = total + ref[...].astype(F32)
    grad = total * gain_ref[...].astype(F32)
    normed = normed_ref[...]
    grad = inverse_ref[:, :1] * (grad - normed * jnp.mean(grad * normed, axis=-1, keepdims=True))
    state_grad_ref[...] = (grad_ref[...].astype(F32) + grad).astype(BF16)
    top = grad.astype(BF16)
    rest = (grad - top.astype(F32)).astype(BF16)
    slot_ref[...] = (mm(high_ref[...], top, TN) + (mm(high_ref[...], rest, TN) + mm(low_ref[...], top, TN))).astype(BF16)


def finish(own, near, normed, inverse, gain, grad_out, high, low):
    rows, width = own.shape
    return pl.pallas_call(
        finish_kernel,
        out_shape=(
            jax.ShapeDtypeStruct((rows, width), BF16),
            jax.ShapeDtypeStruct((high.shape[1], width), BF16),
        ),
        compiler_params=params(18),
        name="finish",
    )(own, *near, normed, inverse, gain, grad_out, high, low)


def shifted(block, axis, step):
    count = lax.axis_size(axis)
    return lax.ppermute(block, axis, [(i, (i + step) % count) for i in range(count)])


def swapped(chunks, axis):
    return [chunks[0]] + [shifted(chunk, axis, step) for step, chunk in enumerate(chunks) if step]


def passed_along(block, axis, distance):
    count = lax.axis_size(axis)
    route = [(i, i + distance) for i in range(count) if 0 <= i + distance < count]
    return lax.ppermute(block, axis, route)


TY = ("x_hi", "y")
TX = ("z", "x_lo", "core")
X = ("x_hi", "x_lo")


def body(
    region_state,
    global_latent,
    send_rows,
    recv_slots,
    regrid_weight,
    window_mask,
    norm_gain,
    w_query,
    w_key,
    w_value,
    w_out,
    out_grad,
):
    state, grad_out = region_state[0, 0], out_grad[0, 0]
    rows, width = state.shape
    gain = norm_gain[None]
    devices = lax.axis_size(TY + TX)
    outgoing = pick_rows(send_rows, global_latent)
    incoming = lax.all_to_all(outgoing, TY + TX, split_axis=0, concat_axis=0, tiled=True)
    normed_in, normed, inverse, high, low = blend_norm(
        recv_slots.reshape(rows, -1), regrid_weight[0, 0], incoming, state, gain
    )
    tiles = (
        normed_in,
        passed_along(normed_in, TY, 1),
        passed_along(normed_in, TY, -1),
        passed_along(normed_in, TX, 1),
        passed_along(normed_in, TX, -1),
    )
    here = {axis: lax.axis_index(axis).reshape(1) for axis in ("z", "y", "core", "x_hi", "x_lo")}
    chunk = width // devices
    halves = [
        attend(half, here["core"], window_mask[0], tiles, grad_out, w_query, w_key, w_value, w_out.T, lax.axis_size("z"))
        for half in range(2)
    ]
    along_z = [swapped(split_sum(here["z"], keep, shifted(send, "core", 1)), "z") for keep, send, *_ in halves]
    attended, dquery, dkey, dvalue = zip(*(half[2:] for half in halves))
    *near, own = spread(dquery, dkey, dvalue, w_query.T, w_key.T, w_value.T)
    returned = (
        passed_along(near[0], TY, -1),
        passed_along(near[1], TY, 1),
        passed_along(near[2], TX, -1),
        passed_along(near[3], TX, 1),
    )
    state_grad, slots = finish(own, returned, normed, inverse, gain, grad_out, high, low)
    sent_back = lax.all_to_all(slots, TY + TX, split_axis=0, concat_axis=0, tiled=True)
    global_grad = add_rows(send_rows, sent_back, global_latent.shape[0])
    along_y = swapped(join_sum(here["y"], *along_z, lax.axis_size("y"), chunk, width), "y")
    total = sum(piece.astype(F32) for piece in along_y).astype(BF16).reshape(-1, 4, chunk, width)
    place = lax.axis_index(X)
    along_x = swapped([lax.dynamic_index_in_dim(total, (place + k) % total.shape[0], 0, keepdims=False) for k in range(total.shape[0])], X)
    weight_grads = sum(piece.astype(F32) for piece in along_x)
    term = jnp.dot(jnp.concatenate(attended, axis=1), w_out, preferred_element_type=F32)
    updated = (state.astype(F32) + term).astype(BF16)
    return (updated[None, None], state_grad[None, None], global_grad, weight_grads)


def solution(mesh):
    ty, tx = mesh.devices.shape
    y, z = max(ty // 2, 1), tx // 4
    fine = jax.sharding.Mesh(mesh.devices.reshape(ty // y, y, z, 2, 2), TY + TX)
    tiles = P(TY, TX)
    flat = P(TY + TX)
    return jax.shard_map(
        body,
        mesh=fine,
        in_specs=(tiles, flat, flat, tiles, tiles, tiles, P(), P(), P(), P(), P(), tiles),
        out_specs=(tiles, tiles, flat, P(None, TY + TX)),
        check_vma=False,
    )
```

```python
import functools
import jax
import jax.numpy as jnp
from jax import lax
from jax.experimental import pallas as pl
from jax.experimental.pallas import tpu as pltpu
from jax.sharding import PartitionSpec as P

HEADS = 8
HEAD_SIZE = 128
EPSILON = 1e-05
LOG2_E = 1.4426950408889634
BF16 = jnp.bfloat16
F32 = jnp.float32
NN = (((1,), (0,)), ((), ()))
NT = (((1,), (1,)), ((), ()))
TN = (((0,), (0,)), ((), ()))


def mm(left, right, dims=NN):
    return lax.dot_general(left, right, dims, preferred_element_type=F32)


def params(mib):
    return pltpu.CompilerParams(vmem_limit_bytes=mib * 1024 * 1024)


def pick_kernel(rows_ref, table_ref, out_ref):
    table_rows = table_ref.shape[0]
    hit = lax.broadcasted_iota(jnp.int32, (table_rows, rows_ref.shape[1]), 0) == rows_ref[...]
    out_ref[...] = mm(hit.astype(F32).astype(BF16), table_ref[...], TN).astype(BF16)


def pick_rows(rows, table):
    count, width, step = rows.shape[1], table.shape[1], 256
    return pl.pallas_call(
        pick_kernel,
        grid=(count // step,),
        in_specs=[
            pl.BlockSpec((1, step), lambda i: (0, i)),
            pl.BlockSpec(table.shape, lambda i: (0, 0)),
        ],
        out_specs=pl.BlockSpec((step, width), lambda i: (i, 0)),
        out_shape=jax.ShapeDtypeStruct((count, width), BF16),
        compiler_params=params(60),
        name="pick_rows",
    )(rows, table)


def add_kernel(rows_ref, sent_ref, out_ref):
    step = out_ref.shape[0]
    ids = lax.broadcasted_iota(jnp.int32, (step, rows_ref.shape[1]), 0) + pl.program_id(0) * step
    hit = (ids == rows_ref[...]).astype(F32).astype(BF16)
    out_ref[...] = mm(hit, sent_ref[...]).astype(BF16)


def add_rows(rows, sent, table_rows):
    step = 256
    return pl.pallas_call(
        add_kernel,
        grid=(table_rows // step,),
        in_specs=[
            pl.BlockSpec(rows.shape, lambda i: (0, 0)),
            pl.BlockSpec(sent.shape, lambda i: (0, 0)),
        ],
        out_specs=pl.BlockSpec((step, sent.shape[1]), lambda i: (i, 0)),
        out_shape=jax.ShapeDtypeStruct((table_rows, sent.shape[1]), BF16),
        compiler_params=params(14),
        name="add_rows",
    )(rows, sent)


def blend_kernel(slots_ref, blend_ref, incoming_ref, state_ref, gain_ref, in_ref, normed_ref, inverse_ref, high_ref, low_ref):
    rows, slots = blend_ref.shape[0], incoming_ref.shape[0]
    lanes = lax.broadcasted_iota(jnp.int32, (rows, slots), 1)
    spread = jnp.zeros((rows, slots), F32)
    for k in range(blend_ref.shape[1]):
        spread = spread + jnp.where(lanes == slots_ref[:, k : k + 1], blend_ref[:, k : k + 1], 0.0)
    high = spread.astype(BF16)
    low = (spread - high.astype(F32)).astype(BF16)
    high_ref[...] = high
    low_ref[...] = low
    incoming = incoming_ref[...]
    pre = state_ref[...].astype(F32) + (mm(high, incoming) + mm(low, incoming))
    inverse = lax.rsqrt(jnp.mean(pre * pre, axis=-1, keepdims=True) + EPSILON)
    normed = pre * inverse
    normed_ref[...] = normed
    inverse_ref[...] = jnp.broadcast_to(inverse, inverse_ref.shape)
    in_ref[...] = (normed * gain_ref[...].astype(F32)).astype(BF16)


def blend_norm(slots, blend, incoming, state, gain):
    rows, width = state.shape
    spread = jax.ShapeDtypeStruct((rows, incoming.shape[0]), BF16)
    return pl.pallas_call(
        blend_kernel,
        out_shape=(
            jax.ShapeDtypeStruct((rows, width), BF16),
            jax.ShapeDtypeStruct((rows, width), F32),
            jax.ShapeDtypeStruct((rows, 128), F32),
            spread,
            spread,
        ),
        compiler_params=params(60),
        name="blend_norm",
    )(slots, blend, incoming, state, gain)


def attend_kernel(
    core_ref, mask_ref, own_ref, up_ref, down_ref, left_ref, right_ref, grad_ref, wq_ref, wk_ref, wv_ref, wo_ref,
    keep_y, send_y, keep_z, send_z, attended_ref, up_grad, down_grad, left_grad, right_grad, own_grad, x_all, x_turned, grads,
):
    step = pl.program_id(0)
    rows = own_ref.shape[0]
    blocks = x_all.shape[0] // rows
    ys, _, _, _, lanes = keep_y.shape
    zs, _, _, piece, _ = keep_z.shape

    @pl.when(step == 0)
    def _():
        for b, ref in enumerate((own_ref, up_ref, down_ref, left_ref, right_ref)):
            x_all[b * rows : (b + 1) * rows] = ref[...]
            x_turned[:, b * rows : (b + 1) * rows] = ref[...].T
        grads[...] = jnp.zeros_like(grads)

    grad_out = grad_ref[...]
    width = grad_out.shape[1]
    scale = HEAD_SIZE ** (-0.5)
    query = mm(own_ref[...], wq_ref[...]).astype(BF16)
    g = mm(grad_out, wo_ref[...], NT).astype(BF16)
    key = mm(x_all[...], wk_ref[...]).astype(BF16)
    value = mm(x_all[...], wv_ref[...]).astype(BF16)
    query_t, g_t = query.T, g.T
    attended_t, dquery_t, dkey, dvalue = [], [], [], []
    for h in range(lanes // HEAD_SIZE):
        at = slice(h * HEAD_SIZE, (h + 1) * HEAD_SIZE)
        raw = mm(key[:, at], query_t[at])
        scores = jnp.concatenate(
            [
                raw[b * rows : (b + 1) * rows] * (scale * LOG2_E) + jnp.where(mask_ref[0, b] > 0, 0.0, -1e30)
                for b in range(blocks)
            ],
            axis=0,
        )
        highest = jnp.max(scores, axis=0, keepdims=True)
        raised = jnp.exp2(scores - highest)
        prob = raised * (1.0 / jnp.sum(raised, axis=0, keepdims=True))
        weights = prob.astype(BF16)
        att = mm(value[:, at], weights, TN).astype(BF16)
        delta = jnp.sum(g_t[at].astype(F32) * att.astype(F32), axis=0, keepdims=True)
        dscore = (prob * (mm(value[:, at], g_t[at]) - delta) * scale).astype(BF16)
        attended_t.append(att)
        dquery_t.append(mm(key[:, at], dscore, TN).astype(BF16))
        dkey.append(mm(dscore, query[:, at]).astype(BF16))
        dvalue.append(mm(weights, g[:, at]).astype(BF16))
    attended_t = jnp.concatenate(attended_t, axis=0)
    dquery = jnp.concatenate(dquery_t, axis=0).T
    dkey = jnp.concatenate(dkey, axis=1)
    dvalue = jnp.concatenate(dvalue, axis=1)
    attended_ref[...] = attended_t.T
    grads[...] += mm(jnp.concatenate([dkey, dvalue], axis=1), jnp.concatenate([wk_ref[...], wv_ref[...]], axis=1), NT)
    grads[:rows] += mm(dquery, wq_ref[...], NT)
    first = core_ref[0] == 0

    def place(keep_ref, send_ref, at, m, where, halves):
        low, high = (half.reshape(-1, lanes) for half in halves)
        keep_ref[at, m, 0, where] = jnp.where(first, low, high).astype(BF16)
        send_ref[at, m, 0, where] = jnp.where(first, high, low).astype(BF16)

    chunk = piece // 16
    every = slice(None)
    for m, part in enumerate((mm(x_turned[:, :rows], dquery), mm(x_turned[...], dkey))):
        part = part.reshape(2, ys, zs, 2, 2, chunk, lanes)
        for y in range(ys):
            place(keep_y, send_y, y, m, every, [part[:, y, :, :, c] for c in range(2)])
    part = mm(x_turned[...], dvalue).reshape(2 * ys, zs, 2, 2, chunk, lanes)
    for z in range(zs):
        place(keep_z, send_z, z, 0, every, [part[:, z, :, c] for c in range(2)])
    part = mm(attended_t, grad_out).reshape(2, zs, 2, 2, chunk, width)
    for z in range(zs):
        for q in range(4):
            columns = slice(q * lanes, (q + 1) * lanes)
            rows_of = slice(q * piece // 4, (q + 1) * piece // 4)
            place(keep_z, send_z, z, 1, rows_of, [part[:, z, :, c, :, columns] for c in range(2)])

    @pl.when(step == pl.num_programs(0) - 1)
    def _():
        own_grad[...] = grads[:rows]
        for b, ref in enumerate((up_grad, down_grad, left_grad, right_grad), 1):
            ref[...] = grads[b * rows : (b + 1) * rows].astype(BF16)


def attend(core, mask, tiles, grad_out, w_query, w_key, w_value, w_out, ys, zs):
    rows, width = grad_out.shape
    near, lanes = len(tiles), 2 * HEAD_SIZE
    steps = width // lanes
    whole = lambda: pl.BlockSpec((rows, width), lambda h: (0, 0), pipeline_mode=pl.Buffered(1))
    columns = lambda: pl.BlockSpec((width, lanes), lambda h: (0, h))
    flags = lambda: pl.BlockSpec(memory_space=pltpu.SMEM)
    parts = lambda n: pl.BlockSpec((n, 2, 1, width // 2 // n, lanes), lambda h: (0, 0, h, 0, 0))
    out = lambda n: pl.BlockSpec((n, lanes), lambda h: (0, h))
    part = lambda n: jax.ShapeDtypeStruct((n, 2, steps, width // 2 // n, lanes), BF16)
    small = jax.ShapeDtypeStruct((rows, width), BF16)
    return pl.pallas_call(
        attend_kernel,
        grid=(steps,),
        in_specs=[flags(), flags()]
        + [whole() for _ in range(near + 1)]
        + [columns(), columns(), columns(), pl.BlockSpec((lanes, width), lambda h: (h, 0))],
        out_specs=[parts(ys), parts(ys), parts(zs), parts(zs), out(rows)]
        + [whole() for _ in range(near)],
        out_shape=(part(ys), part(ys), part(zs), part(zs)) + (small,) * near + (jax.ShapeDtypeStruct((rows, width), F32),),
        scratch_shapes=[
            pltpu.VMEM((near * rows, width), BF16),
            pltpu.VMEM((width, near * rows), BF16),
            pltpu.VMEM((near * rows, width), F32),
        ],
        compiler_params=params(60),
        cost_estimate=pl.CostEstimate(flops=34 * 10**9, bytes_accessed=32 * 10**6, transcendentals=10**6),
        name="attend",
    )(core, mask, *tiles, grad_out, w_query, w_key, w_value, w_out)


def split_kernel(here_ref, keep_ref, came_ref, *out_refs):
    count = len(out_refs)
    for step, ref in enumerate(out_refs):
        at = (here_ref[0] + step) % count
        ref[...] = (keep_ref[at].astype(F32) + came_ref[at].astype(F32)).astype(BF16)


def split_sum(here, keep, came):
    count, mats, steps, *rest = keep.shape
    whole = lambda: pl.BlockSpec((count, mats, 1, *rest), lambda s: (0, 0, s, 0, 0))
    return pl.pallas_call(
        split_kernel,
        grid=(steps,),
        in_specs=[pl.BlockSpec(memory_space=pltpu.SMEM), whole(), whole()],
        out_specs=[pl.BlockSpec((mats, 1, *rest), lambda s: (0, s, 0, 0)) for _ in range(count)],
        out_shape=tuple(jax.ShapeDtypeStruct((mats, steps, *rest), BF16) for _ in range(count)),
        compiler_params=params(60),
        cost_estimate=pl.CostEstimate(flops=10**6, bytes_accessed=6 * 10**6, transcendentals=0),
        name="split_sum",
    )(here, keep, came)


def join_kernel(pieces, out_matrix, here_ref, *refs):
    in_refs, out_refs, table = refs[:pieces], refs[pieces:-1], refs[-1]
    count = len(out_refs)
    chunk = out_refs[0].shape[3]

    def totals():
        for s in range(in_refs[0].shape[1]):
            total = in_refs[0][0, s].astype(F32)
            for ref in in_refs[1:]:
                total = total + ref[0, s].astype(F32)
            yield s, total

    @pl.when(pl.program_id(0) != out_matrix)
    def _():
        for s, total in totals():
            lanes = total.shape[1]
            total = total.reshape(2, count, 2, chunk, lanes)
            for n in range(count):
                table[n, :, :, :, s * lanes : (s + 1) * lanes] = total[:, n]

    if out_matrix >= 0:

        @pl.when(pl.program_id(0) == out_matrix)
        def _():
            for s, total in totals():
                lanes = total.shape[1]
                total = total.reshape(4, 2, 2, chunk, lanes)
                for q in range(4):
                    for y in range(2):
                        table[s % 2 * 2 + y, s // 2, :, :, q * lanes : (q + 1) * lanes] = total[q, y]

    for step, ref in enumerate(out_refs):
        ref[:, :, 0] = table[(here_ref[0] + step) % count].astype(BF16)


def join_sum(here, parts, count, out_matrix, chunk):
    mats, steps, piece, lanes = parts[0].shape
    width = steps * lanes
    return pl.pallas_call(
        functools.partial(join_kernel, len(parts), out_matrix),
        grid=(mats,),
        in_specs=[pl.BlockSpec(memory_space=pltpu.SMEM)]
        + [pl.BlockSpec((1, steps, piece, lanes), lambda m: (m, 0, 0, 0)) for _ in parts],
        out_specs=[pl.BlockSpec((2, 2, 1, chunk, width), lambda m: (0, 0, m, 0, 0)) for _ in range(count)],
        out_shape=tuple(jax.ShapeDtypeStruct((2, 2, mats, chunk, width), BF16) for _ in range(count)),
        scratch_shapes=[pltpu.VMEM((count, 2, 2, chunk, width), F32)],
        compiler_params=params(60),
        cost_estimate=pl.CostEstimate(flops=10**6, bytes_accessed=6 * 10**6, transcendentals=0),
        name="join_sum",
    )(here, *parts)


def finish_kernel(own_ref, up_ref, down_ref, left_ref, right_ref, normed_ref, inverse_ref, gain_ref, grad_ref, high_ref, low_ref, state_grad_ref, slot_ref):
    total = own_ref[...]
    for ref in (up_ref, down_ref, left_ref, right_ref):
        total = total + ref[...].astype(F32)
    grad = total * gain_ref[...].astype(F32)
    normed = normed_ref[...]
    grad = inverse_ref[:, :1] * (grad - normed * jnp.mean(grad * normed, axis=-1, keepdims=True))
    state_grad_ref[...] = (grad_ref[...].astype(F32) + grad).astype(BF16)
    top = grad.astype(BF16)
    rest = (grad - top.astype(F32)).astype(BF16)
    slot_ref[...] = (mm(high_ref[...], top, TN) + (mm(high_ref[...], rest, TN) + mm(low_ref[...], top, TN))).astype(BF16)


def finish(own, near, normed, inverse, gain, grad_out, high, low):
    rows, width = own.shape
    return pl.pallas_call(
        finish_kernel,
        out_shape=(
            jax.ShapeDtypeStruct((rows, width), BF16),
            jax.ShapeDtypeStruct((high.shape[1], width), BF16),
        ),
        compiler_params=params(60),
        name="finish",
    )(own, *near, normed, inverse, gain, grad_out, high, low)


def after(value, others):
    return lax.optimization_barrier((value, others))[0]


def shifted(block, axis, step):
    count = lax.axis_size(axis)
    return lax.ppermute(block, axis, [(i, (i + step) % count) for i in range(count)])


def swapped(chunks, axis):
    return [chunks[0]] + [shifted(chunk, axis, step) for step, chunk in enumerate(chunks) if step]


def passed_along(block, axis, distance):
    count = lax.axis_size(axis)
    route = [(i, i + distance) for i in range(count) if 0 <= i + distance < count]
    return lax.ppermute(block, axis, route)


TY = ("x_hi", "y")
TX = ("z", "x_lo", "core")
X = ("x_hi", "x_lo")


def body(
    region_state,
    global_latent,
    send_rows,
    recv_slots,
    regrid_weight,
    window_mask,
    norm_gain,
    w_query,
    w_key,
    w_value,
    w_out,
    out_grad,
):
    state, grad_out = region_state[0, 0], out_grad[0, 0]
    rows, width = state.shape
    gain = norm_gain[None]
    devices = lax.axis_size(TY + TX)
    outgoing = pick_rows(send_rows, global_latent)
    incoming = lax.all_to_all(outgoing, TY + TX, split_axis=0, concat_axis=0, tiled=True)
    normed_in, normed, inverse, high, low = blend_norm(
        recv_slots.reshape(rows, -1), regrid_weight[0, 0], incoming, state, gain
    )
    tiles = (
        normed_in,
        passed_along(normed_in, TY, 1),
        passed_along(normed_in, TY, -1),
        passed_along(normed_in, TX, 1),
        passed_along(normed_in, TX, -1),
    )
    here = {axis: lax.axis_index(axis).reshape(1) for axis in ("z", "y", "core", "x_hi", "x_lo")}
    chunk = width // devices
    ys, zs = lax.axis_size("y"), lax.axis_size("z")
    keep_y, send_y, keep_z, send_z, attended, *near, own = attend(
        here["core"], window_mask[0], tiles, grad_out, w_query, w_key, w_value, w_out, ys, zs
    )
    came_y, came_z = shifted(send_y, "core", 1), shifted(send_z, "core", 1)
    returned = (
        passed_along(near[0], TY, -1),
        passed_along(near[1], TY, 1),
        passed_along(near[2], TX, -1),
        passed_along(near[3], TX, 1),
    )
    along_z = swapped(split_sum(here["z"], keep_z, came_z), "z")
    along_y = swapped(split_sum(here["y"], keep_y, came_y), "y")
    own = after(own, (along_z[0], along_y[0]))
    state_grad, slots = finish(own, returned, normed, inverse, gain, grad_out, high, low)
    sent_back = lax.all_to_all(after(slots, (along_z, along_y)), TY + TX, split_axis=0, concat_axis=0, tiled=True)
    global_grad = add_rows(send_rows, sent_back, global_latent.shape[0])
    here_y, here_z = after((here["y"], here["z"]), slots)
    second_z = swapped(join_sum(here_z, along_y, zs, -1, chunk), "z")
    second_y = swapped(join_sum(here_y, along_z, ys, 1, chunk), "y")
    total = jnp.concatenate([sum(piece.astype(F32) for piece in group) for group in (second_z, second_y)], axis=2)
    total = total.astype(BF16).reshape(-1, 4, chunk, width)
    term = jnp.dot(attended, w_out, preferred_element_type=F32)
    updated = (state.astype(F32) + term).astype(BF16)
    total = after(total, updated)
    place = lax.axis_index(X)
    along_x = swapped([lax.dynamic_index_in_dim(total, (place + k) % total.shape[0], 0, keepdims=False) for k in range(total.shape[0])], X)
    weight_grads = sum(piece.astype(F32) for piece in after(along_x[:1], global_grad) + along_x[1:])
    return (updated[None, None], state_grad[None, None], global_grad, weight_grads)


def solution(mesh):
    ty, tx = mesh.devices.shape
    y, z = max(ty // 2, 1), tx // 4
    fine = jax.sharding.Mesh(mesh.devices.reshape(ty // y, y, z, 2, 2), TY + TX)
    tiles = P(TY, TX)
    flat = P(TY + TX)
    return jax.shard_map(
        body,
        mesh=fine,
        in_specs=(tiles, flat, flat, tiles, tiles, tiles, P(), P(), P(), P(), P(), tiles),
        out_specs=(tiles, tiles, flat, P(None, TY + TX)),
        check_vma=False,
    )
```

```python
import functools
import jax
import jax.numpy as jnp
from jax import lax
from jax.experimental import pallas as pl
from jax.experimental.pallas import tpu as pltpu
from jax.sharding import PartitionSpec as P

HEADS = 8
HEAD_SIZE = 128
EPSILON = 1e-05
LOG2_E = 1.4426950408889634
BF16 = jnp.bfloat16
F32 = jnp.float32
NN = (((1,), (0,)), ((), ()))
NT = (((1,), (1,)), ((), ()))
TN = (((0,), (0,)), ((), ()))


def mm(left, right, dims=NN):
    return lax.dot_general(left, right, dims, preferred_element_type=F32)


def params(mib):
    return pltpu.CompilerParams(vmem_limit_bytes=mib * 1024 * 1024)


def pick_kernel(rows_ref, table_ref, out_ref):
    table_rows = table_ref.shape[0]
    hit = lax.broadcasted_iota(jnp.int32, (table_rows, rows_ref.shape[1]), 0) == rows_ref[...]
    out_ref[...] = mm(hit.astype(F32).astype(BF16), table_ref[...], TN).astype(BF16)


def pick_rows(rows, table):
    count, width, step = rows.shape[1], table.shape[1], 256
    return pl.pallas_call(
        pick_kernel,
        grid=(count // step,),
        in_specs=[
            pl.BlockSpec((1, step), lambda i: (0, i)),
            pl.BlockSpec(table.shape, lambda i: (0, 0)),
        ],
        out_specs=pl.BlockSpec((step, width), lambda i: (i, 0)),
        out_shape=jax.ShapeDtypeStruct((count, width), BF16),
        compiler_params=params(60),
        name="pick_rows",
    )(rows, table)


def add_kernel(rows_ref, sent_ref, out_ref):
    step = out_ref.shape[0]
    ids = lax.broadcasted_iota(jnp.int32, (step, rows_ref.shape[1]), 0) + pl.program_id(0) * step
    hit = (ids == rows_ref[...]).astype(F32).astype(BF16)
    out_ref[...] = mm(hit, sent_ref[...]).astype(BF16)


def add_rows(rows, sent, table_rows):
    step = 256
    return pl.pallas_call(
        add_kernel,
        grid=(table_rows // step,),
        in_specs=[
            pl.BlockSpec(rows.shape, lambda i: (0, 0)),
            pl.BlockSpec(sent.shape, lambda i: (0, 0)),
        ],
        out_specs=pl.BlockSpec((step, sent.shape[1]), lambda i: (i, 0)),
        out_shape=jax.ShapeDtypeStruct((table_rows, sent.shape[1]), BF16),
        compiler_params=params(14),
        name="add_rows",
    )(rows, sent)


def spread_weights(slots_ref, blend_ref, count):
    rows = blend_ref.shape[0]
    lanes = lax.broadcasted_iota(jnp.int32, (rows, count), 1)
    spread = jnp.zeros((rows, count), F32)
    for k in range(blend_ref.shape[1]):
        spread = spread + jnp.where(lanes == slots_ref[:, k : k + 1], blend_ref[:, k : k + 1], 0.0)
    high = spread.astype(BF16)
    return high, (spread - high.astype(F32)).astype(BF16)


def blend_kernel(slots_ref, blend_ref, incoming_ref, state_ref, gain_ref, in_ref, normed_ref, inverse_ref):
    high, low = spread_weights(slots_ref, blend_ref, incoming_ref.shape[0])
    incoming = incoming_ref[...]
    pre = state_ref[...].astype(F32) + (mm(high, incoming) + mm(low, incoming))
    inverse = lax.rsqrt(jnp.mean(pre * pre, axis=-1, keepdims=True) + EPSILON)
    normed = pre * inverse
    normed_ref[...] = normed
    inverse_ref[...] = jnp.broadcast_to(inverse, inverse_ref.shape)
    in_ref[...] = (normed * gain_ref[...].astype(F32)).astype(BF16)


def blend_norm(slots, blend, incoming, state, gain):
    rows, width = state.shape
    return pl.pallas_call(
        blend_kernel,
        out_shape=(
            jax.ShapeDtypeStruct((rows, width), BF16),
            jax.ShapeDtypeStruct((rows, width), F32),
            jax.ShapeDtypeStruct((rows, 128), F32),
        ),
        compiler_params=params(30),
        name="blend_norm",
    )(slots, blend, incoming, state, gain)


def project_kernel(in_ref, grad_ref, wq_ref, wk_ref, wv_ref, wo_ref, query_ref, key_ref, value_ref, g_ref):
    normed_in = in_ref[...]
    query_ref[...] = mm(normed_in, wq_ref[...]).astype(BF16)
    key_ref[...] = mm(normed_in, wk_ref[...]).astype(BF16)
    value_ref[...] = mm(normed_in, wv_ref[...]).astype(BF16)
    g_ref[...] = mm(grad_ref[...], wo_ref[...], NT).astype(BF16)


def project(normed_in, grad_out, w_query, w_key, w_value, w_out):
    rows, width = normed_in.shape
    lanes = 2 * HEAD_SIZE
    whole = lambda: pl.BlockSpec((rows, width), lambda h: (0, 0), pipeline_mode=pl.Buffered(1))
    columns = lambda n: pl.BlockSpec((n, lanes), lambda h: (0, h))
    return pl.pallas_call(
        project_kernel,
        grid=(width // lanes,),
        in_specs=[whole(), whole()] + [columns(width)] * 3 + [pl.BlockSpec((lanes, width), lambda h: (h, 0))],
        out_specs=[columns(rows)] * 4,
        out_shape=(jax.ShapeDtypeStruct((rows, width), BF16),) * 4,
        compiler_params=params(60),
        cost_estimate=pl.CostEstimate(flops=21 * 10**8, bytes_accessed=11 * 10**6, transcendentals=0),
        name="project",
    )(normed_in, grad_out, w_query, w_key, w_value, w_out)


def attend_kernel(
    core_ref, mask_ref, own_ref, up_ref, down_ref, left_ref, right_ref, grad_ref,
    query_ref, own_key_ref, own_value_ref, g_ref, wq_ref, wk_ref, wv_ref,
    keep_y, send_y, keep_z, send_z, attended_ref, up_grad, down_grad, left_grad, right_grad, own_grad, x_all, x_turned, grads,
):
    step = pl.program_id(0)
    rows = own_ref.shape[0]
    blocks = x_all.shape[0] // rows
    ys, _, _, _, lanes = keep_y.shape
    zs, _, _, piece, _ = keep_z.shape

    @pl.when(step == 0)
    def _():
        for b, ref in enumerate((own_ref, up_ref, down_ref, left_ref, right_ref)):
            x_all[b * rows : (b + 1) * rows] = ref[...]
            x_turned[:, b * rows : (b + 1) * rows] = ref[...].T
        grads[...] = jnp.zeros_like(grads)

    grad_out = grad_ref[...]
    width = grad_out.shape[1]
    scale = HEAD_SIZE ** (-0.5)
    query, g = query_ref[...], g_ref[...]
    near = x_all[rows:]
    key = jnp.concatenate([own_key_ref[...], mm(near, wk_ref[...]).astype(BF16)], axis=0)
    value = jnp.concatenate([own_value_ref[...], mm(near, wv_ref[...]).astype(BF16)], axis=0)
    query_t, g_t = query.T, g.T
    attended_t, dquery_t, dkey, dvalue = [], [], [], []
    for h in range(lanes // HEAD_SIZE):
        at = slice(h * HEAD_SIZE, (h + 1) * HEAD_SIZE)
        raw = mm(key[:, at], query_t[at])
        scores = jnp.concatenate(
            [
                raw[b * rows : (b + 1) * rows] * (scale * LOG2_E) + jnp.where(mask_ref[0, b] > 0, 0.0, -1e30)
                for b in range(blocks)
            ],
            axis=0,
        )
        highest = jnp.max(scores, axis=0, keepdims=True)
        raised = jnp.exp2(scores - highest)
        prob = raised * (1.0 / jnp.sum(raised, axis=0, keepdims=True))
        weights = prob.astype(BF16)
        att = mm(value[:, at], weights, TN).astype(BF16)
        delta = jnp.sum(g_t[at].astype(F32) * att.astype(F32), axis=0, keepdims=True)
        dscore = (prob * (mm(value[:, at], g_t[at]) - delta) * scale).astype(BF16)
        attended_t.append(att)
        dquery_t.append(mm(key[:, at], dscore, TN).astype(BF16))
        dkey.append(mm(dscore, query[:, at]).astype(BF16))
        dvalue.append(mm(weights, g[:, at]).astype(BF16))
    attended_t = jnp.concatenate(attended_t, axis=0)
    dquery = jnp.concatenate(dquery_t, axis=0).T
    dkey = jnp.concatenate(dkey, axis=1)
    dvalue = jnp.concatenate(dvalue, axis=1)
    attended_ref[...] = attended_t.T
    grads[...] += mm(jnp.concatenate([dkey, dvalue], axis=1), jnp.concatenate([wk_ref[...], wv_ref[...]], axis=1), NT)
    grads[:rows] += mm(dquery, wq_ref[...], NT)
    first = core_ref[0] == 0

    def place(keep_ref, send_ref, at, m, where, halves):
        low, high = (half.reshape(-1, lanes) for half in halves)
        keep_ref[at, m, 0, where] = jnp.where(first, low, high).astype(BF16)
        send_ref[at, m, 0, where] = jnp.where(first, high, low).astype(BF16)

    chunk = piece // 16
    every = slice(None)
    for m, part in enumerate((mm(x_turned[:, :rows], dquery), mm(x_turned[...], dkey))):
        part = part.reshape(2, ys, zs, 2, 2, chunk, lanes)
        for y in range(ys):
            place(keep_y, send_y, y, m, every, [part[:, y, :, :, c] for c in range(2)])
    part = mm(x_turned[...], dvalue).reshape(2 * ys, zs, 2, 2, chunk, lanes)
    for z in range(zs):
        place(keep_z, send_z, z, 0, every, [part[:, z, :, c] for c in range(2)])
    part = mm(attended_t, grad_out).reshape(2, zs, 2, 2, chunk, width)
    for z in range(zs):
        for q in range(4):
            columns = slice(q * lanes, (q + 1) * lanes)
            rows_of = slice(q * piece // 4, (q + 1) * piece // 4)
            place(keep_z, send_z, z, 1, rows_of, [part[:, z, :, c, :, columns] for c in range(2)])

    @pl.when(step == pl.num_programs(0) - 1)
    def _():
        own_grad[...] = grads[:rows]
        for b, ref in enumerate((up_grad, down_grad, left_grad, right_grad), 1):
            ref[...] = grads[b * rows : (b + 1) * rows].astype(BF16)


def attend(core, mask, tiles, grad_out, projected, w_query, w_key, w_value, ys, zs):
    rows, width = grad_out.shape
    near, lanes = len(tiles), 2 * HEAD_SIZE
    steps = width // lanes
    whole = lambda: pl.BlockSpec((rows, width), lambda h: (0, 0), pipeline_mode=pl.Buffered(1))
    columns = lambda: pl.BlockSpec((width, lanes), lambda h: (0, h))
    flags = lambda: pl.BlockSpec(memory_space=pltpu.SMEM)
    parts = lambda n: pl.BlockSpec((n, 2, 1, width // 2 // n, lanes), lambda h: (0, 0, h, 0, 0))
    out = lambda n: pl.BlockSpec((n, lanes), lambda h: (0, h))
    part = lambda n: jax.ShapeDtypeStruct((n, 2, steps, width // 2 // n, lanes), BF16)
    small = jax.ShapeDtypeStruct((rows, width), BF16)
    return pl.pallas_call(
        attend_kernel,
        grid=(steps,),
        in_specs=[flags(), flags()]
        + [whole() for _ in range(near + 1)]
        + [out(rows)] * 4
        + [columns()] * 3,
        out_specs=[parts(ys), parts(ys), parts(zs), parts(zs), out(rows)]
        + [whole() for _ in range(near)],
        out_shape=(part(ys), part(ys), part(zs), part(zs)) + (small,) * near + (jax.ShapeDtypeStruct((rows, width), F32),),
        scratch_shapes=[
            pltpu.VMEM((near * rows, width), BF16),
            pltpu.VMEM((width, near * rows), BF16),
            pltpu.VMEM((near * rows, width), F32),
        ],
        compiler_params=params(60),
        cost_estimate=pl.CostEstimate(flops=34 * 10**9, bytes_accessed=32 * 10**6, transcendentals=10**6),
        name="attend",
    )(core, mask, *tiles, grad_out, *projected, w_query, w_key, w_value)


def split_kernel(counts, *refs):
    heres, refs = refs[: len(counts)], refs[len(counts) :]
    in_refs, out_refs = refs[: 2 * len(counts)], list(refs[2 * len(counts) :])
    for group, count in enumerate(counts):
        keep_ref, came_ref = in_refs[2 * group : 2 * group + 2]
        for step in range(count):
            at = (heres[group][0] + step) % count
            out_refs.pop(0)[...] = (keep_ref[at].astype(F32) + came_ref[at].astype(F32)).astype(BF16)


def split_sum(heres, groups):
    counts = tuple(keep.shape[0] for keep, _ in groups)
    steps = groups[0][0].shape[2]
    block = lambda a: pl.BlockSpec((*a.shape[:2], 1, *a.shape[3:]), lambda s: (0, 0, s, 0, 0))
    chunks = [keep.shape[1:] for keep, _ in groups for _ in range(keep.shape[0])]
    out = pl.pallas_call(
        functools.partial(split_kernel, counts),
        grid=(steps,),
        in_specs=[pl.BlockSpec(memory_space=pltpu.SMEM) for _ in heres] + [block(a) for pair in groups for a in pair],
        out_specs=[pl.BlockSpec((c[0], 1, *c[2:]), lambda s: (0, s, 0, 0)) for c in chunks],
        out_shape=tuple(jax.ShapeDtypeStruct(c, BF16) for c in chunks),
        compiler_params=params(60),
        cost_estimate=pl.CostEstimate(flops=10**6, bytes_accessed=12 * 10**6, transcendentals=0),
        name="split_sum",
    )(*heres, *(a for pair in groups for a in pair))
    return out[: counts[0]], out[counts[0] :]


def join_kernel(pieces, out_matrix, here_ref, *refs):
    in_refs, out_refs, table = refs[:pieces], refs[pieces:-1], refs[-1]
    count = len(out_refs)
    chunk = out_refs[0].shape[3]

    def totals():
        for s in range(in_refs[0].shape[1]):
            total = in_refs[0][0, s].astype(F32)
            for ref in in_refs[1:]:
                total = total + ref[0, s].astype(F32)
            yield s, total

    @pl.when(pl.program_id(0) != out_matrix)
    def _():
        for s, total in totals():
            lanes = total.shape[1]
            total = total.reshape(2, count, 2, chunk, lanes)
            for n in range(count):
                table[n, :, :, :, s * lanes : (s + 1) * lanes] = total[:, n]

    if out_matrix >= 0:

        @pl.when(pl.program_id(0) == out_matrix)
        def _():
            for s, total in totals():
                lanes = total.shape[1]
                total = total.reshape(4, 2, 2, chunk, lanes)
                for q in range(4):
                    for y in range(2):
                        table[s % 2 * 2 + y, s // 2, :, :, q * lanes : (q + 1) * lanes] = total[q, y]

    for step, ref in enumerate(out_refs):
        ref[:, :, 0] = table[(here_ref[0] + step) % count].astype(BF16)


def join_sum(here, parts, count, out_matrix, chunk):
    mats, steps, piece, lanes = parts[0].shape
    width = steps * lanes
    return pl.pallas_call(
        functools.partial(join_kernel, len(parts), out_matrix),
        grid=(mats,),
        in_specs=[pl.BlockSpec(memory_space=pltpu.SMEM)]
        + [pl.BlockSpec((1, steps, piece, lanes), lambda m: (m, 0, 0, 0)) for _ in parts],
        out_specs=[pl.BlockSpec((2, 2, 1, chunk, width), lambda m: (0, 0, m, 0, 0)) for _ in range(count)],
        out_shape=tuple(jax.ShapeDtypeStruct((2, 2, mats, chunk, width), BF16) for _ in range(count)),
        scratch_shapes=[pltpu.VMEM((count, 2, 2, chunk, width), F32)],
        compiler_params=params(60),
        cost_estimate=pl.CostEstimate(flops=10**6, bytes_accessed=6 * 10**6, transcendentals=0),
        name="join_sum",
    )(here, *parts)


def finish_kernel(own_ref, up_ref, down_ref, left_ref, right_ref, normed_ref, inverse_ref, gain_ref, grad_ref, slots_ref, blend_ref, state_grad_ref, slot_ref):
    total = own_ref[...]
    for ref in (up_ref, down_ref, left_ref, right_ref):
        total = total + ref[...].astype(F32)
    grad = total * gain_ref[...].astype(F32)
    normed = normed_ref[...]
    grad = inverse_ref[:, :1] * (grad - normed * jnp.mean(grad * normed, axis=-1, keepdims=True))
    state_grad_ref[...] = (grad_ref[...].astype(F32) + grad).astype(BF16)
    top = grad.astype(BF16)
    rest = (grad - top.astype(F32)).astype(BF16)
    high, low = spread_weights(slots_ref, blend_ref, slot_ref.shape[0])
    slot_ref[...] = (mm(high, top, TN) + (mm(high, rest, TN) + mm(low, top, TN))).astype(BF16)


def finish(own, near, normed, inverse, gain, grad_out, slots, blend, count):
    rows, width = own.shape
    return pl.pallas_call(
        finish_kernel,
        out_shape=(
            jax.ShapeDtypeStruct((rows, width), BF16),
            jax.ShapeDtypeStruct((count, width), BF16),
        ),
        compiler_params=params(60),
        name="finish",
    )(own, *near, normed, inverse, gain, grad_out, slots, blend)


def after(value, others):
    return lax.optimization_barrier((value, others))[0]


def shifted(block, axis, step):
    count = lax.axis_size(axis)
    return lax.ppermute(block, axis, [(i, (i + step) % count) for i in range(count)])


def swapped(chunks, axis):
    return [chunks[0]] + [shifted(chunk, axis, step) for step, chunk in enumerate(chunks) if step]


def passed_along(block, axis, distance):
    count = lax.axis_size(axis)
    route = [(i, i + distance) for i in range(count) if 0 <= i + distance < count]
    return lax.ppermute(block, axis, route)


TY = ("x_hi", "y")
TX = ("z", "x_lo", "core")
X = ("x_hi", "x_lo")


def body(
    region_state,
    global_latent,
    send_rows,
    recv_slots,
    regrid_weight,
    window_mask,
    norm_gain,
    w_query,
    w_key,
    w_value,
    w_out,
    out_grad,
):
    state, grad_out = region_state[0, 0], out_grad[0, 0]
    rows, width = state.shape
    gain = norm_gain[None]
    devices = lax.axis_size(TY + TX)
    outgoing = pick_rows(send_rows, global_latent)
    incoming = lax.all_to_all(outgoing, TY + TX, split_axis=0, concat_axis=0, tiled=True)
    slot_ids, blend = recv_slots.reshape(rows, -1), regrid_weight[0, 0]
    normed_in, normed, inverse = blend_norm(slot_ids, blend, incoming, state, gain)
    tiles = (
        normed_in,
        passed_along(normed_in, TY, 1),
        passed_along(normed_in, TY, -1),
        passed_along(normed_in, TX, 1),
        passed_along(normed_in, TX, -1),
    )
    projected = project(normed_in, grad_out, w_query, w_key, w_value, w_out)
    here = {axis: lax.axis_index(axis).reshape(1) for axis in ("z", "y", "core", "x_hi", "x_lo")}
    chunk = width // devices
    ys, zs = lax.axis_size("y"), lax.axis_size("z")
    keep_y, send_y, keep_z, send_z, attended, *near, own = attend(
        here["core"], window_mask[0], tiles, grad_out, projected, w_query, w_key, w_value, ys, zs
    )
    came_y, came_z = shifted(send_y, "core", 1), shifted(send_z, "core", 1)
    returned = (
        passed_along(near[0], TY, -1),
        passed_along(near[1], TY, 1),
        passed_along(near[2], TX, -1),
        passed_along(near[3], TX, 1),
    )
    chunks_y, chunks_z = split_sum((here["y"], here["z"]), ((keep_y, came_y), (keep_z, came_z)))
    along_y, along_z = swapped(chunks_y, "y"), swapped(chunks_z, "z")
    own = after(own, (along_z[0], along_y[0]))
    state_grad, slots = finish(own, returned, normed, inverse, gain, grad_out, slot_ids, blend, incoming.shape[0])
    term = jnp.dot(after(attended, slots), w_out, preferred_element_type=F32)
    updated = (state.astype(F32) + term).astype(BF16)
    sent_back = lax.all_to_all(after(slots, (along_z, along_y, updated)), TY + TX, split_axis=0, concat_axis=0, tiled=True)
    global_grad = add_rows(send_rows, sent_back, global_latent.shape[0])
    here_y, here_z = after((here["y"], here["z"]), slots)
    second_z = swapped(join_sum(here_z, along_y, zs, -1, chunk), "z")
    second_y = swapped(join_sum(here_y, along_z, ys, 1, chunk), "y")
    total = jnp.concatenate([sum(piece.astype(F32) for piece in group) for group in (second_z, second_y)], axis=2)
    total = total.astype(BF16).reshape(-1, 4, chunk, width)
    place = lax.axis_index(X)
    along_x = swapped([lax.dynamic_index_in_dim(total, (place + k) % total.shape[0], 0, keepdims=False) for k in range(total.shape[0])], X)
    weight_grads = sum(piece.astype(F32) for piece in after(along_x[:1], global_grad) + along_x[1:])
    return (updated[None, None], state_grad[None, None], global_grad, weight_grads)


def solution(mesh):
    ty, tx = mesh.devices.shape
    y, z = max(ty // 2, 1), tx // 4
    fine = jax.sharding.Mesh(mesh.devices.reshape(ty // y, y, z, 2, 2), TY + TX)
    tiles = P(TY, TX)
    flat = P(TY + TX)
    return jax.shard_map(
        body,
        mesh=fine,
        in_specs=(tiles, flat, flat, tiles, tiles, tiles, P(), P(), P(), P(), P(), tiles),
        out_specs=(tiles, tiles, flat, P(None, TY + TX)),
        check_vma=False,
    )
```

```python
import functools
import jax
import jax.numpy as jnp
from jax import lax
from jax.experimental import pallas as pl
from jax.experimental.pallas import tpu as pltpu
from jax.sharding import PartitionSpec as P

HEADS = 8
HEAD_SIZE = 128
EPSILON = 1e-05
LOG2_E = 1.4426950408889634
BF16 = jnp.bfloat16
F32 = jnp.float32
NN = (((1,), (0,)), ((), ()))
NT = (((1,), (1,)), ((), ()))
TN = (((0,), (0,)), ((), ()))


def mm(left, right, dims=NN):
    return lax.dot_general(left, right, dims, preferred_element_type=F32)


def params(mib):
    return pltpu.CompilerParams(vmem_limit_bytes=mib * 1024 * 1024)


def pick_kernel(rows_ref, table_ref, out_ref):
    table_rows = table_ref.shape[0]
    hit = lax.broadcasted_iota(jnp.int32, (table_rows, rows_ref.shape[1]), 0) == rows_ref[...]
    out_ref[...] = mm(hit.astype(F32).astype(BF16), table_ref[...], TN).astype(BF16)


def pick_rows(rows, table):
    count, width, step = rows.shape[1], table.shape[1], 256
    return pl.pallas_call(
        pick_kernel,
        grid=(count // step,),
        in_specs=[
            pl.BlockSpec((1, step), lambda i: (0, i)),
            pl.BlockSpec(table.shape, lambda i: (0, 0)),
        ],
        out_specs=pl.BlockSpec((step, width), lambda i: (i, 0)),
        out_shape=jax.ShapeDtypeStruct((count, width), BF16),
        compiler_params=params(60),
        name="pick_rows",
    )(rows, table)


def add_kernel(rows_ref, sent_ref, out_ref):
    step = out_ref.shape[0]
    ids = lax.broadcasted_iota(jnp.int32, (step, rows_ref.shape[1]), 0) + pl.program_id(0) * step
    hit = (ids == rows_ref[...]).astype(F32).astype(BF16)
    out_ref[...] = mm(hit, sent_ref[...]).astype(BF16)


def add_rows(rows, sent, table_rows):
    step = 256
    return pl.pallas_call(
        add_kernel,
        grid=(table_rows // step,),
        in_specs=[
            pl.BlockSpec(rows.shape, lambda i: (0, 0)),
            pl.BlockSpec(sent.shape, lambda i: (0, 0)),
        ],
        out_specs=pl.BlockSpec((step, sent.shape[1]), lambda i: (i, 0)),
        out_shape=jax.ShapeDtypeStruct((table_rows, sent.shape[1]), BF16),
        compiler_params=params(14),
        name="add_rows",
    )(rows, sent)


def spread_weights(slots_ref, blend_ref, count):
    rows = blend_ref.shape[0]
    lanes = lax.broadcasted_iota(jnp.int32, (rows, count), 1)
    spread = jnp.zeros((rows, count), F32)
    for k in range(blend_ref.shape[1]):
        spread = spread + jnp.where(lanes == slots_ref[:, k : k + 1], blend_ref[:, k : k + 1], 0.0)
    high = spread.astype(BF16)
    return high, (spread - high.astype(F32)).astype(BF16)


def blend_kernel(slots_ref, blend_ref, incoming_ref, state_ref, gain_ref, in_ref, normed_ref, inverse_ref):
    high, low = spread_weights(slots_ref, blend_ref, incoming_ref.shape[0])
    incoming = incoming_ref[...]
    pre = state_ref[...].astype(F32) + (mm(high, incoming) + mm(low, incoming))
    inverse = lax.rsqrt(jnp.mean(pre * pre, axis=-1, keepdims=True) + EPSILON)
    normed = pre * inverse
    normed_ref[...] = normed
    inverse_ref[...] = jnp.broadcast_to(inverse, inverse_ref.shape)
    in_ref[...] = (normed * gain_ref[...].astype(F32)).astype(BF16)


def blend_norm(slots, blend, incoming, state, gain):
    rows, width = state.shape
    return pl.pallas_call(
        blend_kernel,
        out_shape=(
            jax.ShapeDtypeStruct((rows, width), BF16),
            jax.ShapeDtypeStruct((rows, width), F32),
            jax.ShapeDtypeStruct((rows, 128), F32),
        ),
        compiler_params=params(30),
        name="blend_norm",
    )(slots, blend, incoming, state, gain)


def project_kernel(in_ref, grad_ref, wq_ref, wk_ref, wv_ref, wo_ref, query_ref, key_ref, value_ref, g_ref):
    normed_in = in_ref[...]
    query_ref[...] = mm(normed_in, wq_ref[...]).astype(BF16)
    key_ref[...] = mm(normed_in, wk_ref[...]).astype(BF16)
    value_ref[...] = mm(normed_in, wv_ref[...]).astype(BF16)
    g_ref[...] = mm(grad_ref[...], wo_ref[...], NT).astype(BF16)


def project(normed_in, grad_out, w_query, w_key, w_value, w_out):
    rows, width = normed_in.shape
    lanes = 2 * HEAD_SIZE
    whole = lambda: pl.BlockSpec((rows, width), lambda h: (0, 0), pipeline_mode=pl.Buffered(1))
    columns = lambda n: pl.BlockSpec((n, lanes), lambda h: (0, h))
    return pl.pallas_call(
        project_kernel,
        grid=(width // lanes,),
        in_specs=[whole(), whole()] + [columns(width)] * 3 + [pl.BlockSpec((lanes, width), lambda h: (h, 0))],
        out_specs=[columns(rows)] * 4,
        out_shape=(jax.ShapeDtypeStruct((rows, width), BF16),) * 4,
        compiler_params=params(60),
        cost_estimate=pl.CostEstimate(flops=21 * 10**8, bytes_accessed=11 * 10**6, transcendentals=0),
        name="project",
    )(normed_in, grad_out, w_query, w_key, w_value, w_out)


def attend_kernel(
    core_ref, mask_ref, own_ref, left_ref, right_ref, up_ref, down_ref, grad_ref,
    query_ref, own_key_ref, own_value_ref, g_ref, wq_ref, wk_ref, wv_ref,
    keep_y, send_y, keep_z, send_z, attended_ref, up_grad, down_grad, left_grad, right_grad, own_grad, x_all, x_turned, grads,
):
    step = pl.program_id(0)
    rows = own_ref.shape[0]
    blocks = x_all.shape[0] // rows
    ys, _, _, _, lanes = keep_y.shape
    zs, _, _, piece, _ = keep_z.shape

    @pl.when(step == 0)
    def _():
        for b, ref in enumerate((own_ref, up_ref, down_ref, left_ref, right_ref)):
            x_all[b * rows : (b + 1) * rows] = ref[...]
            x_turned[:, b * rows : (b + 1) * rows] = ref[...].T
        grads[...] = jnp.zeros_like(grads)

    grad_out = grad_ref[...]
    width = grad_out.shape[1]
    scale = HEAD_SIZE ** (-0.5)
    query, g = query_ref[...], g_ref[...]
    near = x_all[rows:]
    key = jnp.concatenate([own_key_ref[...], mm(near, wk_ref[...]).astype(BF16)], axis=0)
    value = jnp.concatenate([own_value_ref[...], mm(near, wv_ref[...]).astype(BF16)], axis=0)
    query_t, g_t = query.T, g.T
    attended_t, dquery_t, dkey, dvalue = [], [], [], []
    for h in range(lanes // HEAD_SIZE):
        at = slice(h * HEAD_SIZE, (h + 1) * HEAD_SIZE)
        raw = mm(key[:, at], query_t[at])
        scores = jnp.concatenate(
            [
                raw[b * rows : (b + 1) * rows] * (scale * LOG2_E) + jnp.where(mask_ref[0, b] > 0, 0.0, -1e30)
                for b in range(blocks)
            ],
            axis=0,
        )
        highest = jnp.max(scores, axis=0, keepdims=True)
        raised = jnp.exp2(scores - highest)
        prob = raised * (1.0 / jnp.sum(raised, axis=0, keepdims=True))
        weights = prob.astype(BF16)
        att = mm(value[:, at], weights, TN).astype(BF16)
        delta = jnp.sum(g_t[at].astype(F32) * att.astype(F32), axis=0, keepdims=True)
        dscore = (prob * (mm(value[:, at], g_t[at]) - delta) * scale).astype(BF16)
        attended_t.append(att)
        dquery_t.append(mm(key[:, at], dscore, TN).astype(BF16))
        dkey.append(mm(dscore, query[:, at]).astype(BF16))
        dvalue.append(mm(weights, g[:, at]).astype(BF16))
    attended_t = jnp.concatenate(attended_t, axis=0)
    dquery = jnp.concatenate(dquery_t, axis=0).T
    dkey = jnp.concatenate(dkey, axis=1)
    dvalue = jnp.concatenate(dvalue, axis=1)
    attended_ref[...] = attended_t.T
    grads[...] += mm(jnp.concatenate([dkey, dvalue], axis=1), jnp.concatenate([wk_ref[...], wv_ref[...]], axis=1), NT)
    grads[:rows] += mm(dquery, wq_ref[...], NT)
    first = core_ref[0] == 0

    def place(keep_ref, send_ref, at, m, where, halves):
        low, high = (half.reshape(-1, lanes) for half in halves)
        keep_ref[at, m, 0, where] = jnp.where(first, low, high).astype(BF16)
        send_ref[at, m, 0, where] = jnp.where(first, high, low).astype(BF16)

    chunk = piece // 16
    every = slice(None)
    for m, part in enumerate((mm(x_turned[:, :rows], dquery), mm(x_turned[...], dkey))):
        part = part.reshape(2, ys, zs, 2, 2, chunk, lanes)
        for y in range(ys):
            place(keep_y, send_y, y, m, every, [part[:, y, :, :, c] for c in range(2)])
    part = mm(x_turned[...], dvalue).reshape(2 * ys, zs, 2, 2, chunk, lanes)
    for z in range(zs):
        place(keep_z, send_z, z, 0, every, [part[:, z, :, c] for c in range(2)])
    part = mm(attended_t, grad_out).reshape(2, zs, 2, 2, chunk, width)
    for z in range(zs):
        for q in range(4):
            columns = slice(q * lanes, (q + 1) * lanes)
            rows_of = slice(q * piece // 4, (q + 1) * piece // 4)
            place(keep_z, send_z, z, 1, rows_of, [part[:, z, :, c, :, columns] for c in range(2)])

    @pl.when(step == pl.num_programs(0) - 1)
    def _():
        own_grad[...] = grads[:rows]
        for b, ref in enumerate((up_grad, down_grad, left_grad, right_grad), 1):
            ref[...] = grads[b * rows : (b + 1) * rows].astype(BF16)


def attend(core, mask, tiles, grad_out, projected, w_query, w_key, w_value, ys, zs):
    rows, width = grad_out.shape
    near, lanes = len(tiles), 2 * HEAD_SIZE
    own, up, down, left, right = tiles
    steps = width // lanes
    whole = lambda: pl.BlockSpec((rows, width), lambda h: (0, 0), pipeline_mode=pl.Buffered(1))
    columns = lambda: pl.BlockSpec((width, lanes), lambda h: (0, h))
    flags = lambda: pl.BlockSpec(memory_space=pltpu.SMEM)
    parts = lambda n: pl.BlockSpec((n, 2, 1, width // 2 // n, lanes), lambda h: (0, 0, h, 0, 0))
    out = lambda n: pl.BlockSpec((n, lanes), lambda h: (0, h))
    part = lambda n: jax.ShapeDtypeStruct((n, 2, steps, width // 2 // n, lanes), BF16)
    small = jax.ShapeDtypeStruct((rows, width), BF16)
    return pl.pallas_call(
        attend_kernel,
        grid=(steps,),
        in_specs=[flags(), flags()]
        + [whole() for _ in range(near + 1)]
        + [out(rows)] * 4
        + [columns()] * 3,
        out_specs=[parts(ys), parts(ys), parts(zs), parts(zs), out(rows)]
        + [whole() for _ in range(near)],
        out_shape=(part(ys), part(ys), part(zs), part(zs)) + (small,) * near + (jax.ShapeDtypeStruct((rows, width), F32),),
        scratch_shapes=[
            pltpu.VMEM((near * rows, width), BF16),
            pltpu.VMEM((width, near * rows), BF16),
            pltpu.VMEM((near * rows, width), F32),
        ],
        compiler_params=params(60),
        cost_estimate=pl.CostEstimate(flops=34 * 10**9, bytes_accessed=32 * 10**6, transcendentals=10**6),
        name="attend",
    )(core, mask, own, left, right, up, down, grad_out, *projected, w_query, w_key, w_value)


def split_kernel(counts, *refs):
    heres, refs = refs[: len(counts)], refs[len(counts) :]
    in_refs, out_refs = refs[: 2 * len(counts)], list(refs[2 * len(counts) :])
    for group, count in enumerate(counts):
        keep_ref, came_ref = in_refs[2 * group : 2 * group + 2]
        for step in range(count):
            at = (heres[group][0] + step) % count
            out_refs.pop(0)[...] = (keep_ref[at].astype(F32) + came_ref[at].astype(F32)).astype(BF16)


def split_sum(heres, groups):
    counts = tuple(keep.shape[0] for keep, _ in groups)
    steps = groups[0][0].shape[2]
    block = lambda a: pl.BlockSpec((*a.shape[:2], 1, *a.shape[3:]), lambda s: (0, 0, s, 0, 0))
    chunks = [keep.shape[1:] for keep, _ in groups for _ in range(keep.shape[0])]
    out = pl.pallas_call(
        functools.partial(split_kernel, counts),
        grid=(steps,),
        in_specs=[pl.BlockSpec(memory_space=pltpu.SMEM) for _ in heres] + [block(a) for pair in groups for a in pair],
        out_specs=[pl.BlockSpec((c[0], 1, *c[2:]), lambda s: (0, s, 0, 0)) for c in chunks],
        out_shape=tuple(jax.ShapeDtypeStruct(c, BF16) for c in chunks),
        compiler_params=params(60),
        cost_estimate=pl.CostEstimate(flops=10**6, bytes_accessed=12 * 10**6, transcendentals=0),
        name="split_sum",
    )(*heres, *(a for pair in groups for a in pair))
    return out[: counts[0]], out[counts[0] :]


def join_kernel(pieces, out_matrix, here_ref, *refs):
    in_refs, out_refs, table = refs[:pieces], refs[pieces:-1], refs[-1]
    count = len(out_refs)
    chunk = out_refs[0].shape[3]

    def totals():
        for s in range(in_refs[0].shape[1]):
            total = in_refs[0][0, s].astype(F32)
            for ref in in_refs[1:]:
                total = total + ref[0, s].astype(F32)
            yield s, total

    @pl.when(pl.program_id(0) != out_matrix)
    def _():
        for s, total in totals():
            lanes = total.shape[1]
            total = total.reshape(2, count, 2, chunk, lanes)
            for n in range(count):
                table[n, :, :, :, s * lanes : (s + 1) * lanes] = total[:, n]

    if out_matrix >= 0:

        @pl.when(pl.program_id(0) == out_matrix)
        def _():
            for s, total in totals():
                lanes = total.shape[1]
                total = total.reshape(4, 2, 2, chunk, lanes)
                for q in range(4):
                    for y in range(2):
                        table[s % 2 * 2 + y, s // 2, :, :, q * lanes : (q + 1) * lanes] = total[q, y]

    for step, ref in enumerate(out_refs):
        ref[:, :, 0] = table[(here_ref[0] + step) % count].astype(BF16)


def join_sum(here, parts, count, out_matrix, chunk):
    mats, steps, piece, lanes = parts[0].shape
    width = steps * lanes
    return pl.pallas_call(
        functools.partial(join_kernel, len(parts), out_matrix),
        grid=(mats,),
        in_specs=[pl.BlockSpec(memory_space=pltpu.SMEM)]
        + [pl.BlockSpec((1, steps, piece, lanes), lambda m: (m, 0, 0, 0)) for _ in parts],
        out_specs=[pl.BlockSpec((2, 2, 1, chunk, width), lambda m: (0, 0, m, 0, 0)) for _ in range(count)],
        out_shape=tuple(jax.ShapeDtypeStruct((2, 2, mats, chunk, width), BF16) for _ in range(count)),
        scratch_shapes=[pltpu.VMEM((count, 2, 2, chunk, width), F32)],
        compiler_params=params(60),
        cost_estimate=pl.CostEstimate(flops=10**6, bytes_accessed=6 * 10**6, transcendentals=0),
        name="join_sum",
    )(here, *parts)


def finish_kernel(own_ref, up_ref, down_ref, left_ref, right_ref, normed_ref, inverse_ref, gain_ref, grad_ref, slots_ref, blend_ref, state_grad_ref, slot_ref):
    total = own_ref[...]
    for ref in (up_ref, down_ref, left_ref, right_ref):
        total = total + ref[...].astype(F32)
    grad = total * gain_ref[...].astype(F32)
    normed = normed_ref[...]
    grad = inverse_ref[:, :1] * (grad - normed * jnp.mean(grad * normed, axis=-1, keepdims=True))
    state_grad_ref[...] = (grad_ref[...].astype(F32) + grad).astype(BF16)
    top = grad.astype(BF16)
    rest = (grad - top.astype(F32)).astype(BF16)
    high, low = spread_weights(slots_ref, blend_ref, slot_ref.shape[0])
    slot_ref[...] = (mm(high, top, TN) + (mm(high, rest, TN) + mm(low, top, TN))).astype(BF16)


def finish(own, near, normed, inverse, gain, grad_out, slots, blend, count):
    rows, width = own.shape
    return pl.pallas_call(
        finish_kernel,
        out_shape=(
            jax.ShapeDtypeStruct((rows, width), BF16),
            jax.ShapeDtypeStruct((count, width), BF16),
        ),
        compiler_params=params(60),
        name="finish",
    )(own, *near, normed, inverse, gain, grad_out, slots, blend)


def after(value, others):
    return lax.optimization_barrier((value, others))[0]


def shifted(block, axis, step):
    count = lax.axis_size(axis)
    return lax.ppermute(block, axis, [(i, (i + step) % count) for i in range(count)])


def swapped(chunks, axis):
    return [chunks[0]] + [shifted(chunk, axis, step) for step, chunk in enumerate(chunks) if step]


def passed_along(block, axis, distance):
    count = lax.axis_size(axis)
    route = [(i, i + distance) for i in range(count) if 0 <= i + distance < count]
    return lax.ppermute(block, axis, route)


TY = ("x_hi", "y")
TX = ("z", "x_lo", "core")
X = ("x_hi", "x_lo")


def body(
    region_state,
    global_latent,
    send_rows,
    recv_slots,
    regrid_weight,
    window_mask,
    norm_gain,
    w_query,
    w_key,
    w_value,
    w_out,
    out_grad,
):
    state, grad_out = region_state[0, 0], out_grad[0, 0]
    rows, width = state.shape
    gain = norm_gain[None]
    devices = lax.axis_size(TY + TX)
    outgoing = pick_rows(send_rows, global_latent)
    incoming = lax.all_to_all(outgoing, TY + TX, split_axis=0, concat_axis=0, tiled=True)
    slot_ids, blend = recv_slots.reshape(rows, -1), regrid_weight[0, 0]
    normed_in, normed, inverse = blend_norm(slot_ids, blend, incoming, state, gain)
    tiles = (
        normed_in,
        passed_along(normed_in, TY, 1),
        passed_along(normed_in, TY, -1),
        passed_along(normed_in, TX, 1),
        passed_along(normed_in, TX, -1),
    )
    projected = project(normed_in, grad_out, w_query, w_key, w_value, w_out)
    here = {axis: lax.axis_index(axis).reshape(1) for axis in ("z", "y", "core", "x_hi", "x_lo")}
    chunk = width // devices
    ys, zs = lax.axis_size("y"), lax.axis_size("z")
    keep_y, send_y, keep_z, send_z, attended, *near, own = attend(
        here["core"], window_mask[0], tiles, grad_out, projected, w_query, w_key, w_value, ys, zs
    )
    came_y, came_z = shifted(send_y, "core", 1), shifted(send_z, "core", 1)
    returned = (
        passed_along(near[0], TY, -1),
        passed_along(near[1], TY, 1),
        passed_along(near[2], TX, -1),
        passed_along(near[3], TX, 1),
    )
    chunks_y, chunks_z = split_sum((here["y"], here["z"]), ((keep_y, came_y), (keep_z, came_z)))
    along_y, along_z = swapped(chunks_y, "y"), swapped(chunks_z, "z")
    own = after(own, (along_z[0], along_y[0]))
    state_grad, slots = finish(own, returned, normed, inverse, gain, grad_out, slot_ids, blend, incoming.shape[0])
    term = jnp.dot(after(attended, slots), w_out, preferred_element_type=F32)
    updated = (state.astype(F32) + term).astype(BF16)
    here_y, here_z = after((here["y"], here["z"]), slots)
    second_y = swapped(join_sum(here_y, along_z, ys, 1, chunk), "y")
    sent = after(slots, (along_y, updated, second_y[1]))
    sent_back = lax.all_to_all(sent, TY + TX, split_axis=0, concat_axis=0, tiled=True)
    global_grad = add_rows(send_rows, sent_back, global_latent.shape[0])
    second_z = swapped(join_sum(here_z, along_y, zs, -1, chunk), "z")
    total = jnp.concatenate([sum(piece.astype(F32) for piece in group) for group in (second_z, second_y)], axis=2)
    total = total.astype(BF16).reshape(-1, 4, chunk, width)
    place = lax.axis_index(X)
    along_x = swapped([lax.dynamic_index_in_dim(total, (place + k) % total.shape[0], 0, keepdims=False) for k in range(total.shape[0])], X)
    weight_grads = sum(piece.astype(F32) for piece in after(along_x[:1], global_grad) + along_x[1:])
    return (updated[None, None], state_grad[None, None], global_grad, weight_grads)


def solution(mesh):
    ty, tx = mesh.devices.shape
    y, z = max(ty // 2, 1), tx // 4
    fine = jax.sharding.Mesh(mesh.devices.reshape(ty // y, y, z, 2, 2), TY + TX)
    tiles = P(TY, TX)
    flat = P(TY + TX)
    return jax.shard_map(
        body,
        mesh=fine,
        in_specs=(tiles, flat, flat, tiles, tiles, tiles, P(), P(), P(), P(), P(), tiles),
        out_specs=(tiles, tiles, flat, P(None, TY + TX)),
        check_vma=False,
    )
```

```python
import functools
import jax
import jax.numpy as jnp
from jax import lax
from jax.experimental import pallas as pl
from jax.experimental.pallas import tpu as pltpu
from jax.sharding import PartitionSpec as P

HEADS = 8
HEAD_SIZE = 128
EPSILON = 1e-05
LOG2_E = 1.4426950408889634
BF16 = jnp.bfloat16
F32 = jnp.float32
NN = (((1,), (0,)), ((), ()))
NT = (((1,), (1,)), ((), ()))
TN = (((0,), (0,)), ((), ()))


def mm(left, right, dims=NN):
    return lax.dot_general(left, right, dims, preferred_element_type=F32)


def params(mib):
    return pltpu.CompilerParams(vmem_limit_bytes=mib * 1024 * 1024)


def pick_kernel(rows_ref, table_ref, out_ref):
    table_rows = table_ref.shape[0]
    hit = lax.broadcasted_iota(jnp.int32, (table_rows, rows_ref.shape[1]), 0) == rows_ref[...]
    out_ref[...] = mm(hit.astype(F32).astype(BF16), table_ref[...], TN).astype(BF16)


def pick_rows(rows, table):
    count, width, step = rows.shape[1], table.shape[1], 512
    return pl.pallas_call(
        pick_kernel,
        grid=(count // step,),
        in_specs=[
            pl.BlockSpec((1, step), lambda i: (0, i)),
            pl.BlockSpec(table.shape, lambda i: (0, 0)),
        ],
        out_specs=pl.BlockSpec((step, width), lambda i: (i, 0)),
        out_shape=jax.ShapeDtypeStruct((count, width), BF16),
        compiler_params=params(60),
        name="pick_rows",
    )(rows, table)


def add_kernel(rows_ref, sent_ref, out_ref):
    step = out_ref.shape[0]
    ids = lax.broadcasted_iota(jnp.int32, (step, rows_ref.shape[1]), 0) + pl.program_id(0) * step
    hit = (ids == rows_ref[...]).astype(F32).astype(BF16)
    out_ref[...] = mm(hit, sent_ref[...]).astype(BF16)


def add_rows(rows, sent, table_rows):
    step = 256
    return pl.pallas_call(
        add_kernel,
        grid=(table_rows // step,),
        in_specs=[
            pl.BlockSpec(rows.shape, lambda i: (0, 0)),
            pl.BlockSpec(sent.shape, lambda i: (0, 0)),
        ],
        out_specs=pl.BlockSpec((step, sent.shape[1]), lambda i: (i, 0)),
        out_shape=jax.ShapeDtypeStruct((table_rows, sent.shape[1]), BF16),
        compiler_params=params(14),
        name="add_rows",
    )(rows, sent)


def spread_weights(slots_ref, blend_ref, count):
    rows = blend_ref.shape[0]
    lanes = lax.broadcasted_iota(jnp.int32, (rows, count), 1)
    spread = jnp.zeros((rows, count), F32)
    for k in range(blend_ref.shape[1]):
        spread = spread + jnp.where(lanes == slots_ref[:, k : k + 1], blend_ref[:, k : k + 1], 0.0)
    high = spread.astype(BF16)
    return high, (spread - high.astype(F32)).astype(BF16)


def blend_kernel(slots_ref, blend_ref, incoming_ref, state_ref, gain_ref, in_ref, normed_ref, inverse_ref):
    high, low = spread_weights(slots_ref, blend_ref, incoming_ref.shape[0])
    incoming = incoming_ref[...]
    pre = state_ref[...].astype(F32) + (mm(high, incoming) + mm(low, incoming))
    inverse = lax.rsqrt(jnp.mean(pre * pre, axis=-1, keepdims=True) + EPSILON)
    normed = pre * inverse
    normed_ref[...] = normed
    inverse_ref[...] = jnp.broadcast_to(inverse, inverse_ref.shape)
    in_ref[...] = (normed * gain_ref[...].astype(F32)).astype(BF16)


def blend_norm(slots, blend, incoming, state, gain):
    rows, width = state.shape
    return pl.pallas_call(
        blend_kernel,
        out_shape=(
            jax.ShapeDtypeStruct((rows, width), BF16),
            jax.ShapeDtypeStruct((rows, width), F32),
            jax.ShapeDtypeStruct((rows, 128), F32),
        ),
        compiler_params=params(30),
        name="blend_norm",
    )(slots, blend, incoming, state, gain)


def project_kernel(in_ref, grad_ref, wq_ref, wk_ref, wv_ref, wo_ref, query_ref, key_ref, value_ref, g_ref):
    normed_in = in_ref[...]
    query_ref[...] = mm(normed_in, wq_ref[...]).astype(BF16)
    key_ref[...] = mm(normed_in, wk_ref[...]).astype(BF16)
    value_ref[...] = mm(normed_in, wv_ref[...]).astype(BF16)
    g_ref[...] = mm(grad_ref[...], wo_ref[...], NT).astype(BF16)


def project(normed_in, grad_out, w_query, w_key, w_value, w_out):
    rows, width = normed_in.shape
    lanes = 2 * HEAD_SIZE
    whole = lambda: pl.BlockSpec((rows, width), lambda h: (0, 0), pipeline_mode=pl.Buffered(1))
    columns = lambda n: pl.BlockSpec((n, lanes), lambda h: (0, h))
    return pl.pallas_call(
        project_kernel,
        grid=(width // lanes,),
        in_specs=[whole(), whole()] + [columns(width)] * 3 + [pl.BlockSpec((lanes, width), lambda h: (h, 0))],
        out_specs=[columns(rows)] * 4,
        out_shape=(jax.ShapeDtypeStruct((rows, width), BF16),) * 4,
        compiler_params=params(60),
        cost_estimate=pl.CostEstimate(flops=21 * 10**8, bytes_accessed=11 * 10**6, transcendentals=0),
        name="project",
    )(normed_in, grad_out, w_query, w_key, w_value, w_out)


def attend_kernel(
    core_ref, mask_ref, own_ref, left_ref, right_ref, up_ref, down_ref, grad_ref,
    query_ref, own_key_ref, own_value_ref, g_ref, wq_ref, wk_ref, wv_ref,
    keep_y, send_y, keep_z, send_z, attended_ref, up_grad, down_grad, left_grad, right_grad, own_grad, x_all, x_turned, grads,
):
    step = pl.program_id(0)
    rows = own_ref.shape[0]
    blocks = x_all.shape[0] // rows
    ys, _, _, _, lanes = keep_y.shape
    zs, _, _, piece, _ = keep_z.shape

    @pl.when(step == 0)
    def _():
        for b, ref in enumerate((own_ref, up_ref, down_ref, left_ref, right_ref)):
            x_all[b * rows : (b + 1) * rows] = ref[...]
            x_turned[:, b * rows : (b + 1) * rows] = ref[...].T
        grads[...] = jnp.zeros_like(grads)

    grad_out = grad_ref[...]
    width = grad_out.shape[1]
    scale = HEAD_SIZE ** (-0.5)
    query, g = query_ref[...], g_ref[...]
    near = x_all[rows:]
    key = jnp.concatenate([own_key_ref[...], mm(near, wk_ref[...]).astype(BF16)], axis=0)
    value = jnp.concatenate([own_value_ref[...], mm(near, wv_ref[...]).astype(BF16)], axis=0)
    query_t, g_t = query.T, g.T
    attended_t, dquery_t, dkey, dvalue = [], [], [], []
    for h in range(lanes // HEAD_SIZE):
        at = slice(h * HEAD_SIZE, (h + 1) * HEAD_SIZE)
        raw = mm(key[:, at], query_t[at])
        scores = jnp.concatenate(
            [
                raw[b * rows : (b + 1) * rows] * (scale * LOG2_E) + jnp.where(mask_ref[0, b] > 0, 0.0, -1e30)
                for b in range(blocks)
            ],
            axis=0,
        )
        highest = jnp.max(scores, axis=0, keepdims=True)
        raised = jnp.exp2(scores - highest)
        prob = raised * (1.0 / jnp.sum(raised, axis=0, keepdims=True))
        weights = prob.astype(BF16)
        att = mm(value[:, at], weights, TN).astype(BF16)
        delta = jnp.sum(g_t[at].astype(F32) * att.astype(F32), axis=0, keepdims=True)
        dscore = (prob * (mm(value[:, at], g_t[at]) - delta) * scale).astype(BF16)
        attended_t.append(att)
        dquery_t.append(mm(key[:, at], dscore, TN).astype(BF16))
        dkey.append(mm(dscore, query[:, at]).astype(BF16))
        dvalue.append(mm(weights, g[:, at]).astype(BF16))
    attended_t = jnp.concatenate(attended_t, axis=0)
    dquery = jnp.concatenate(dquery_t, axis=0).T
    dkey = jnp.concatenate(dkey, axis=1)
    dvalue = jnp.concatenate(dvalue, axis=1)
    attended_ref[...] = attended_t.T
    grads[...] += mm(jnp.concatenate([dkey, dvalue], axis=1), jnp.concatenate([wk_ref[...], wv_ref[...]], axis=1), NT)
    grads[:rows] += mm(dquery, wq_ref[...], NT)
    first = core_ref[0] == 0

    def place(keep_ref, send_ref, at, m, where, halves):
        low, high = (half.reshape(-1, lanes) for half in halves)
        keep_ref[at, m, 0, where] = jnp.where(first, low, high).astype(BF16)
        send_ref[at, m, 0, where] = jnp.where(first, high, low).astype(BF16)

    chunk = piece // 16
    every = slice(None)
    for m, part in enumerate((mm(x_turned[:, :rows], dquery), mm(x_turned[...], dkey))):
        part = part.reshape(2, ys, zs, 2, 2, chunk, lanes)
        for y in range(ys):
            place(keep_y, send_y, y, m, every, [part[:, y, :, :, c] for c in range(2)])
    part = mm(x_turned[...], dvalue).reshape(2 * ys, zs, 2, 2, chunk, lanes)
    for z in range(zs):
        place(keep_z, send_z, z, 0, every, [part[:, z, :, c] for c in range(2)])
    part = mm(attended_t, grad_out).reshape(2, zs, 2, 2, chunk, width)
    for z in range(zs):
        for q in range(4):
            columns = slice(q * lanes, (q + 1) * lanes)
            rows_of = slice(q * piece // 4, (q + 1) * piece // 4)
            place(keep_z, send_z, z, 1, rows_of, [part[:, z, :, c, :, columns] for c in range(2)])

    @pl.when(step == pl.num_programs(0) - 1)
    def _():
        own_grad[...] = grads[:rows]
        for b, ref in enumerate((up_grad, down_grad, left_grad, right_grad), 1):
            ref[...] = grads[b * rows : (b + 1) * rows].astype(BF16)


def attend(core, mask, tiles, grad_out, projected, w_query, w_key, w_value, ys, zs):
    rows, width = grad_out.shape
    near, lanes = len(tiles), 2 * HEAD_SIZE
    own, up, down, left, right = tiles
    steps = width // lanes
    whole = lambda: pl.BlockSpec((rows, width), lambda h: (0, 0), pipeline_mode=pl.Buffered(1))
    columns = lambda: pl.BlockSpec((width, lanes), lambda h: (0, h))
    flags = lambda: pl.BlockSpec(memory_space=pltpu.SMEM)
    parts = lambda n: pl.BlockSpec((n, 2, 1, width // 2 // n, lanes), lambda h: (0, 0, h, 0, 0))
    out = lambda n: pl.BlockSpec((n, lanes), lambda h: (0, h))
    part = lambda n: jax.ShapeDtypeStruct((n, 2, steps, width // 2 // n, lanes), BF16)
    small = jax.ShapeDtypeStruct((rows, width), BF16)
    return pl.pallas_call(
        attend_kernel,
        grid=(steps,),
        in_specs=[flags(), flags()]
        + [whole() for _ in range(near + 1)]
        + [out(rows)] * 4
        + [columns()] * 3,
        out_specs=[parts(ys), parts(ys), parts(zs), parts(zs), out(rows)]
        + [whole() for _ in range(near)],
        out_shape=(part(ys), part(ys), part(zs), part(zs)) + (small,) * near + (jax.ShapeDtypeStruct((rows, width), F32),),
        scratch_shapes=[
            pltpu.VMEM((near * rows, width), BF16),
            pltpu.VMEM((width, near * rows), BF16),
            pltpu.VMEM((near * rows, width), F32),
        ],
        compiler_params=params(60),
        cost_estimate=pl.CostEstimate(flops=34 * 10**9, bytes_accessed=32 * 10**6, transcendentals=10**6),
        name="attend",
    )(core, mask, own, left, right, up, down, grad_out, *projected, w_query, w_key, w_value)


def split_kernel(counts, *refs):
    heres, refs = refs[: len(counts)], refs[len(counts) :]
    in_refs, out_refs = refs[: 2 * len(counts)], list(refs[2 * len(counts) :])
    for group, count in enumerate(counts):
        keep_ref, came_ref = in_refs[2 * group : 2 * group + 2]
        for step in range(count):
            at = (heres[group][0] + step) % count
            out_refs.pop(0)[...] = (keep_ref[at].astype(F32) + came_ref[at].astype(F32)).astype(BF16)


def split_sum(heres, groups):
    counts = tuple(keep.shape[0] for keep, _ in groups)
    steps = groups[0][0].shape[2]
    block = lambda a: pl.BlockSpec((*a.shape[:2], 1, *a.shape[3:]), lambda s: (0, 0, s, 0, 0))
    chunks = [keep.shape[1:] for keep, _ in groups for _ in range(keep.shape[0])]
    out = pl.pallas_call(
        functools.partial(split_kernel, counts),
        grid=(steps,),
        in_specs=[pl.BlockSpec(memory_space=pltpu.SMEM) for _ in heres] + [block(a) for pair in groups for a in pair],
        out_specs=[pl.BlockSpec((c[0], 1, *c[2:]), lambda s: (0, s, 0, 0)) for c in chunks],
        out_shape=tuple(jax.ShapeDtypeStruct(c, BF16) for c in chunks),
        compiler_params=params(60),
        cost_estimate=pl.CostEstimate(flops=10**6, bytes_accessed=12 * 10**6, transcendentals=0),
        name="split_sum",
    )(*heres, *(a for pair in groups for a in pair))
    return out[: counts[0]], out[counts[0] :]


def join_kernel(pieces, out_matrix, here_ref, *refs):
    in_refs, out_refs, table = refs[:pieces], refs[pieces:-1], refs[-1]
    count = len(out_refs)
    chunk = out_refs[0].shape[3]

    def totals():
        for s in range(in_refs[0].shape[1]):
            total = in_refs[0][0, s].astype(F32)
            for ref in in_refs[1:]:
                total = total + ref[0, s].astype(F32)
            yield s, total

    @pl.when(pl.program_id(0) != out_matrix)
    def _():
        for s, total in totals():
            lanes = total.shape[1]
            total = total.reshape(2, count, 2, chunk, lanes)
            for n in range(count):
                table[n, :, :, :, s * lanes : (s + 1) * lanes] = total[:, n]

    if out_matrix >= 0:

        @pl.when(pl.program_id(0) == out_matrix)
        def _():
            for s, total in totals():
                lanes = total.shape[1]
                total = total.reshape(4, 2, 2, chunk, lanes)
                for q in range(4):
                    for y in range(2):
                        table[s % 2 * 2 + y, s // 2, :, :, q * lanes : (q + 1) * lanes] = total[q, y]

    for step, ref in enumerate(out_refs):
        ref[:, :, 0] = table[(here_ref[0] + step) % count].astype(BF16)


def join_sum(here, parts, count, out_matrix, chunk):
    mats, steps, piece, lanes = parts[0].shape
    width = steps * lanes
    return pl.pallas_call(
        functools.partial(join_kernel, len(parts), out_matrix),
        grid=(mats,),
        in_specs=[pl.BlockSpec(memory_space=pltpu.SMEM)]
        + [pl.BlockSpec((1, steps, piece, lanes), lambda m: (m, 0, 0, 0)) for _ in parts],
        out_specs=[pl.BlockSpec((2, 2, 1, chunk, width), lambda m: (0, 0, m, 0, 0)) for _ in range(count)],
        out_shape=tuple(jax.ShapeDtypeStruct((2, 2, mats, chunk, width), BF16) for _ in range(count)),
        scratch_shapes=[pltpu.VMEM((count, 2, 2, chunk, width), F32)],
        compiler_params=params(60),
        cost_estimate=pl.CostEstimate(flops=10**6, bytes_accessed=6 * 10**6, transcendentals=0),
        name="join_sum",
    )(here, *parts)


def finish_kernel(own_ref, up_ref, down_ref, left_ref, right_ref, normed_ref, inverse_ref, gain_ref, grad_ref, slots_ref, blend_ref, state_grad_ref, slot_ref):
    total = own_ref[...]
    for ref in (up_ref, down_ref, left_ref, right_ref):
        total = total + ref[...].astype(F32)
    grad = total * gain_ref[...].astype(F32)
    normed = normed_ref[...]
    grad = inverse_ref[:, :1] * (grad - normed * jnp.mean(grad * normed, axis=-1, keepdims=True))
    state_grad_ref[...] = (grad_ref[...].astype(F32) + grad).astype(BF16)
    top = grad.astype(BF16)
    rest = (grad - top.astype(F32)).astype(BF16)
    high, low = spread_weights(slots_ref, blend_ref, slot_ref.shape[0])
    slot_ref[...] = (mm(high, top, TN) + (mm(high, rest, TN) + mm(low, top, TN))).astype(BF16)


def finish(own, near, normed, inverse, gain, grad_out, slots, blend, count):
    rows, width = own.shape
    return pl.pallas_call(
        finish_kernel,
        out_shape=(
            jax.ShapeDtypeStruct((rows, width), BF16),
            jax.ShapeDtypeStruct((count, width), BF16),
        ),
        compiler_params=params(26),
        name="finish",
    )(own, *near, normed, inverse, gain, grad_out, slots, blend)


def after(value, others):
    return lax.optimization_barrier((value, others))[0]


def shifted(block, axis, step):
    count = lax.axis_size(axis)
    return lax.ppermute(block, axis, [(i, (i + step) % count) for i in range(count)])


def swapped(chunks, axis):
    return [chunks[0]] + [shifted(chunk, axis, step) for step, chunk in enumerate(chunks) if step]


def passed_along(block, axis, distance):
    count = lax.axis_size(axis)
    route = [(i, i + distance) for i in range(count) if 0 <= i + distance < count]
    return lax.ppermute(block, axis, route)


TY = ("x_hi", "y")
TX = ("z", "x_lo", "core")
X = ("x_hi", "x_lo")


def body(
    region_state,
    global_latent,
    send_rows,
    recv_slots,
    regrid_weight,
    window_mask,
    norm_gain,
    w_query,
    w_key,
    w_value,
    w_out,
    out_grad,
):
    state, grad_out = region_state[0, 0], out_grad[0, 0]
    rows, width = state.shape
    gain = norm_gain[None]
    devices = lax.axis_size(TY + TX)
    outgoing = pick_rows(send_rows, global_latent)
    incoming = lax.all_to_all(outgoing, TY + TX, split_axis=0, concat_axis=0, tiled=True)
    slot_ids, blend = recv_slots.reshape(rows, -1), regrid_weight[0, 0]
    normed_in, normed, inverse = blend_norm(slot_ids, blend, incoming, state, gain)
    tiles = (
        normed_in,
        passed_along(normed_in, TY, 1),
        passed_along(normed_in, TY, -1),
        passed_along(normed_in, TX, 1),
        passed_along(normed_in, TX, -1),
    )
    projected = project(normed_in, grad_out, w_query, w_key, w_value, w_out)
    here = {axis: lax.axis_index(axis).reshape(1) for axis in ("z", "y", "core", "x_hi", "x_lo")}
    chunk = width // devices
    ys, zs = lax.axis_size("y"), lax.axis_size("z")
    keep_y, send_y, keep_z, send_z, attended, *near, own = attend(
        here["core"], window_mask[0], tiles, grad_out, projected, w_query, w_key, w_value, ys, zs
    )
    came_y, came_z = shifted(send_y, "core", 1), shifted(send_z, "core", 1)
    returned = (
        passed_along(near[0], TY, -1),
        passed_along(near[1], TY, 1),
        passed_along(near[2], TX, -1),
        passed_along(near[3], TX, 1),
    )
    chunks_y, chunks_z = split_sum((here["y"], here["z"]), ((keep_y, came_y), (keep_z, came_z)))
    along_y, along_z = swapped(chunks_y, "y"), swapped(chunks_z, "z")
    own = after(own, (along_z[0], along_y[0]))
    state_grad, slots = finish(own, returned, normed, inverse, gain, grad_out, slot_ids, blend, incoming.shape[0])
    term = jnp.dot(after(attended, slots), w_out, preferred_element_type=F32)
    updated = (state.astype(F32) + term).astype(BF16)
    here_y, here_z = after((here["y"], here["z"]), slots)
    second_y = swapped(join_sum(here_y, along_z, ys, 1, chunk), "y")
    sent = after(slots, (along_y, updated, second_y[1]))
    sent_back = lax.all_to_all(sent, TY + TX, split_axis=0, concat_axis=0, tiled=True)
    global_grad = add_rows(send_rows, sent_back, global_latent.shape[0])
    second_z = swapped(join_sum(here_z, along_y, zs, -1, chunk), "z")
    total = jnp.concatenate([sum(piece.astype(F32) for piece in group) for group in (second_z, second_y)], axis=2)
    total = total.astype(BF16).reshape(-1, 4, chunk, width)
    place = lax.axis_index(X)
    along_x = swapped([lax.dynamic_index_in_dim(total, (place + k) % total.shape[0], 0, keepdims=False) for k in range(total.shape[0])], X)
    weight_grads = sum(piece.astype(F32) for piece in after(along_x[:1], global_grad) + along_x[1:])
    return (updated[None, None], state_grad[None, None], global_grad, weight_grads)


def solution(mesh):
    ty, tx = mesh.devices.shape
    y, z = max(ty // 2, 1), tx // 4
    fine = jax.sharding.Mesh(mesh.devices.reshape(ty // y, y, z, 2, 2), TY + TX)
    tiles = P(TY, TX)
    flat = P(TY + TX)
    return jax.shard_map(
        body,
        mesh=fine,
        in_specs=(tiles, flat, flat, tiles, tiles, tiles, P(), P(), P(), P(), P(), tiles),
        out_specs=(tiles, tiles, flat, P(None, TY + TX)),
        check_vma=False,
    )
```

```python
import functools
import jax
import jax.numpy as jnp
from jax import lax
from jax.experimental import pallas as pl
from jax.experimental.pallas import tpu as pltpu
from jax.sharding import PartitionSpec as P

HEADS = 8
HEAD_SIZE = 128
EPSILON = 1e-05
LOG2_E = 1.4426950408889634
BF16 = jnp.bfloat16
F32 = jnp.float32
NN = (((1,), (0,)), ((), ()))
NT = (((1,), (1,)), ((), ()))
TN = (((0,), (0,)), ((), ()))


def mm(left, right, dims=NN):
    return lax.dot_general(left, right, dims, preferred_element_type=F32)


def params(mib):
    return pltpu.CompilerParams(vmem_limit_bytes=mib * 1024 * 1024)


def pick_kernel(rows_ref, table_ref, out_ref):
    table_rows = table_ref.shape[0]
    hit = lax.broadcasted_iota(jnp.int32, (table_rows, rows_ref.shape[1]), 0) == rows_ref[...]
    out_ref[...] = mm(hit.astype(F32).astype(BF16), table_ref[...], TN).astype(BF16)


def pick_rows(rows, table):
    count, width, step = rows.shape[1], table.shape[1], 512
    return pl.pallas_call(
        pick_kernel,
        grid=(count // step,),
        in_specs=[
            pl.BlockSpec((1, step), lambda i: (0, i)),
            pl.BlockSpec(table.shape, lambda i: (0, 0)),
        ],
        out_specs=pl.BlockSpec((step, width), lambda i: (i, 0)),
        out_shape=jax.ShapeDtypeStruct((count, width), BF16),
        compiler_params=params(60),
        name="pick_rows",
    )(rows, table)


def add_kernel(rows_ref, sent_ref, out_ref):
    step = out_ref.shape[0]
    ids = lax.broadcasted_iota(jnp.int32, (step, rows_ref.shape[1]), 0) + pl.program_id(0) * step
    hit = (ids == rows_ref[...]).astype(F32).astype(BF16)
    out_ref[...] = mm(hit, sent_ref[...]).astype(BF16)


def add_rows(rows, sent, table_rows):
    step = 256
    return pl.pallas_call(
        add_kernel,
        grid=(table_rows // step,),
        in_specs=[
            pl.BlockSpec(rows.shape, lambda i: (0, 0)),
            pl.BlockSpec(sent.shape, lambda i: (0, 0)),
        ],
        out_specs=pl.BlockSpec((step, sent.shape[1]), lambda i: (i, 0)),
        out_shape=jax.ShapeDtypeStruct((table_rows, sent.shape[1]), BF16),
        compiler_params=params(14),
        name="add_rows",
    )(rows, sent)


def spread_weights(slots_ref, blend_ref, count):
    rows = blend_ref.shape[0]
    lanes = lax.broadcasted_iota(jnp.int32, (rows, count), 1)
    spread = jnp.zeros((rows, count), F32)
    for k in range(blend_ref.shape[1]):
        spread = spread + jnp.where(lanes == slots_ref[:, k : k + 1], blend_ref[:, k : k + 1], 0.0)
    high = spread.astype(BF16)
    return high, (spread - high.astype(F32)).astype(BF16)


def blend_kernel(slots_ref, blend_ref, incoming_ref, state_ref, gain_ref, in_ref, normed_ref, inverse_ref):
    high, low = spread_weights(slots_ref, blend_ref, incoming_ref.shape[0])
    incoming = incoming_ref[...]
    pre = state_ref[...].astype(F32) + (mm(high, incoming) + mm(low, incoming))
    inverse = lax.rsqrt(jnp.mean(pre * pre, axis=-1, keepdims=True) + EPSILON)
    normed = pre * inverse
    normed_ref[...] = normed
    inverse_ref[...] = jnp.broadcast_to(inverse, inverse_ref.shape)
    in_ref[...] = (normed * gain_ref[...].astype(F32)).astype(BF16)


def blend_norm(slots, blend, incoming, state, gain):
    rows, width = state.shape
    return pl.pallas_call(
        blend_kernel,
        out_shape=(
            jax.ShapeDtypeStruct((rows, width), BF16),
            jax.ShapeDtypeStruct((rows, width), F32),
            jax.ShapeDtypeStruct((rows, 128), F32),
        ),
        compiler_params=params(30),
        name="blend_norm",
    )(slots, blend, incoming, state, gain)


def project_kernel(in_ref, grad_ref, wq_ref, wk_ref, wv_ref, wo_ref, query_ref, key_ref, value_ref, g_ref):
    normed_in = in_ref[...]
    query_ref[...] = mm(normed_in, wq_ref[...]).astype(BF16)
    key_ref[...] = mm(normed_in, wk_ref[...]).astype(BF16)
    value_ref[...] = mm(normed_in, wv_ref[...]).astype(BF16)
    g_ref[...] = mm(grad_ref[...], wo_ref[...], NT).astype(BF16)


def project(normed_in, grad_out, w_query, w_key, w_value, w_out):
    rows, width = normed_in.shape
    lanes = 2 * HEAD_SIZE
    whole = lambda: pl.BlockSpec((rows, width), lambda h: (0, 0), pipeline_mode=pl.Buffered(1))
    columns = lambda n: pl.BlockSpec((n, lanes), lambda h: (0, h))
    return pl.pallas_call(
        project_kernel,
        grid=(width // lanes,),
        in_specs=[whole(), whole()] + [columns(width)] * 3 + [pl.BlockSpec((lanes, width), lambda h: (h, 0))],
        out_specs=[columns(rows)] * 4,
        out_shape=(jax.ShapeDtypeStruct((rows, width), BF16),) * 4,
        compiler_params=params(60),
        cost_estimate=pl.CostEstimate(flops=21 * 10**8, bytes_accessed=11 * 10**6, transcendentals=0),
        name="project",
    )(normed_in, grad_out, w_query, w_key, w_value, w_out)


def sides_kernel(left_ref, right_ref, wk_ref, wv_ref, key_ref, value_ref):
    rows = left_ref.shape[0]
    for at, ref in ((0, left_ref), (rows, right_ref)):
        key_ref[at : at + rows] = mm(ref[...], wk_ref[...]).astype(BF16)
        value_ref[at : at + rows] = mm(ref[...], wv_ref[...]).astype(BF16)


def sides(left, right, w_key, w_value):
    rows, width = left.shape
    lanes = 2 * HEAD_SIZE
    whole = lambda: pl.BlockSpec((rows, width), lambda h: (0, 0), pipeline_mode=pl.Buffered(1))
    columns = lambda n: pl.BlockSpec((n, lanes), lambda h: (0, h))
    return pl.pallas_call(
        sides_kernel,
        grid=(width // lanes,),
        in_specs=[whole(), whole(), columns(width), columns(width)],
        out_specs=[columns(2 * rows)] * 2,
        out_shape=(jax.ShapeDtypeStruct((2 * rows, width), BF16),) * 2,
        compiler_params=params(60),
        cost_estimate=pl.CostEstimate(flops=21 * 10**8, bytes_accessed=8 * 10**6, transcendentals=0),
        name="sides",
    )(left, right, w_key, w_value)


def attend_kernel(
    core_ref, mask_ref, own_ref, left_ref, right_ref, up_ref, down_ref, grad_ref,
    query_ref, own_key_ref, own_value_ref, g_ref, side_key_ref, side_value_ref, wq_ref, wk_ref, wv_ref,
    keep_y, send_y, keep_z, send_z, attended_ref, up_grad, down_grad, left_grad, right_grad, own_grad, x_all, x_turned, grads,
):
    step = pl.program_id(0)
    rows = own_ref.shape[0]
    blocks = x_all.shape[0] // rows
    ys, _, _, _, lanes = keep_y.shape
    zs, _, _, piece, _ = keep_z.shape

    @pl.when(step == 0)
    def _():
        for b, ref in enumerate((own_ref, up_ref, down_ref, left_ref, right_ref)):
            x_all[b * rows : (b + 1) * rows] = ref[...]
            x_turned[:, b * rows : (b + 1) * rows] = ref[...].T
        grads[...] = jnp.zeros_like(grads)

    grad_out = grad_ref[...]
    width = grad_out.shape[1]
    scale = HEAD_SIZE ** (-0.5)
    query, g = query_ref[...], g_ref[...]
    near = x_all[rows : 3 * rows]
    key = jnp.concatenate([own_key_ref[...], mm(near, wk_ref[...]).astype(BF16), side_key_ref[...]], axis=0)
    value = jnp.concatenate([own_value_ref[...], mm(near, wv_ref[...]).astype(BF16), side_value_ref[...]], axis=0)
    query_t, g_t = query.T, g.T
    attended_t, dquery_t, dkey, dvalue = [], [], [], []
    for h in range(lanes // HEAD_SIZE):
        at = slice(h * HEAD_SIZE, (h + 1) * HEAD_SIZE)
        raw = mm(key[:, at], query_t[at])
        scores = jnp.concatenate(
            [
                raw[b * rows : (b + 1) * rows] * (scale * LOG2_E) + jnp.where(mask_ref[0, b] > 0, 0.0, -1e30)
                for b in range(blocks)
            ],
            axis=0,
        )
        highest = jnp.max(scores, axis=0, keepdims=True)
        raised = jnp.exp2(scores - highest)
        prob = raised * (1.0 / jnp.sum(raised, axis=0, keepdims=True))
        weights = prob.astype(BF16)
        att = mm(value[:, at], weights, TN).astype(BF16)
        delta = jnp.sum(g_t[at].astype(F32) * att.astype(F32), axis=0, keepdims=True)
        dscore = (prob * (mm(value[:, at], g_t[at]) - delta) * scale).astype(BF16)
        attended_t.append(att)
        dquery_t.append(mm(key[:, at], dscore, TN).astype(BF16))
        dkey.append(mm(dscore, query[:, at]).astype(BF16))
        dvalue.append(mm(weights, g[:, at]).astype(BF16))
    attended_t = jnp.concatenate(attended_t, axis=0)
    dquery = jnp.concatenate(dquery_t, axis=0).T
    dkey = jnp.concatenate(dkey, axis=1)
    dvalue = jnp.concatenate(dvalue, axis=1)
    attended_ref[...] = attended_t.T
    grads[...] += mm(jnp.concatenate([dkey, dvalue], axis=1), jnp.concatenate([wk_ref[...], wv_ref[...]], axis=1), NT)
    grads[:rows] += mm(dquery, wq_ref[...], NT)
    first = core_ref[0] == 0

    def place(keep_ref, send_ref, at, m, where, halves):
        low, high = (half.reshape(-1, lanes) for half in halves)
        keep_ref[at, m, 0, where] = jnp.where(first, low, high).astype(BF16)
        send_ref[at, m, 0, where] = jnp.where(first, high, low).astype(BF16)

    chunk = piece // 16
    every = slice(None)
    for m, part in enumerate((mm(x_turned[:, :rows], dquery), mm(x_turned[...], dkey))):
        part = part.reshape(2, ys, zs, 2, 2, chunk, lanes)
        for y in range(ys):
            place(keep_y, send_y, y, m, every, [part[:, y, :, :, c] for c in range(2)])
    part = mm(x_turned[...], dvalue).reshape(2 * ys, zs, 2, 2, chunk, lanes)
    for z in range(zs):
        place(keep_z, send_z, z, 0, every, [part[:, z, :, c] for c in range(2)])
    part = mm(attended_t, grad_out).reshape(2, zs, 2, 2, chunk, width)
    for z in range(zs):
        for q in range(4):
            columns = slice(q * lanes, (q + 1) * lanes)
            rows_of = slice(q * piece // 4, (q + 1) * piece // 4)
            place(keep_z, send_z, z, 1, rows_of, [part[:, z, :, c, :, columns] for c in range(2)])

    @pl.when(step == pl.num_programs(0) - 1)
    def _():
        own_grad[...] = grads[:rows]
        for b, ref in enumerate((up_grad, down_grad, left_grad, right_grad), 1):
            ref[...] = grads[b * rows : (b + 1) * rows].astype(BF16)


def attend(core, mask, tiles, grad_out, projected, w_query, w_key, w_value, ys, zs):
    rows, width = grad_out.shape
    near, lanes = len(tiles), 2 * HEAD_SIZE
    own, up, down, left, right = tiles
    steps = width // lanes
    whole = lambda: pl.BlockSpec((rows, width), lambda h: (0, 0), pipeline_mode=pl.Buffered(1))
    columns = lambda: pl.BlockSpec((width, lanes), lambda h: (0, h))
    flags = lambda: pl.BlockSpec(memory_space=pltpu.SMEM)
    parts = lambda n: pl.BlockSpec((n, 2, 1, width // 2 // n, lanes), lambda h: (0, 0, h, 0, 0))
    out = lambda n: pl.BlockSpec((n, lanes), lambda h: (0, h))
    part = lambda n: jax.ShapeDtypeStruct((n, 2, steps, width // 2 // n, lanes), BF16)
    small = jax.ShapeDtypeStruct((rows, width), BF16)
    return pl.pallas_call(
        attend_kernel,
        grid=(steps,),
        in_specs=[flags(), flags()]
        + [whole() for _ in range(near + 1)]
        + [out(rows)] * 4
        + [out(2 * rows)] * 2
        + [columns()] * 3,
        out_specs=[parts(ys), parts(ys), parts(zs), parts(zs), out(rows)]
        + [whole() for _ in range(near)],
        out_shape=(part(ys), part(ys), part(zs), part(zs)) + (small,) * near + (jax.ShapeDtypeStruct((rows, width), F32),),
        scratch_shapes=[
            pltpu.VMEM((near * rows, width), BF16),
            pltpu.VMEM((width, near * rows), BF16),
            pltpu.VMEM((near * rows, width), F32),
        ],
        compiler_params=params(60),
        cost_estimate=pl.CostEstimate(flops=34 * 10**9, bytes_accessed=32 * 10**6, transcendentals=10**6),
        name="attend",
    )(core, mask, own, left, right, up, down, grad_out, *projected, w_query, w_key, w_value)


def split_kernel(counts, *refs):
    heres, refs = refs[: len(counts)], refs[len(counts) :]
    in_refs, out_refs = refs[: 2 * len(counts)], list(refs[2 * len(counts) :])
    for group, count in enumerate(counts):
        keep_ref, came_ref = in_refs[2 * group : 2 * group + 2]
        for step in range(count):
            at = (heres[group][0] + step) % count
            out_refs.pop(0)[...] = (keep_ref[at].astype(F32) + came_ref[at].astype(F32)).astype(BF16)


def split_sum(heres, groups):
    counts = tuple(keep.shape[0] for keep, _ in groups)
    steps = groups[0][0].shape[2]
    block = lambda a: pl.BlockSpec((*a.shape[:2], 1, *a.shape[3:]), lambda s: (0, 0, s, 0, 0))
    chunks = [keep.shape[1:] for keep, _ in groups for _ in range(keep.shape[0])]
    out = pl.pallas_call(
        functools.partial(split_kernel, counts),
        grid=(steps,),
        in_specs=[pl.BlockSpec(memory_space=pltpu.SMEM) for _ in heres] + [block(a) for pair in groups for a in pair],
        out_specs=[pl.BlockSpec((c[0], 1, *c[2:]), lambda s: (0, s, 0, 0)) for c in chunks],
        out_shape=tuple(jax.ShapeDtypeStruct(c, BF16) for c in chunks),
        compiler_params=params(60),
        cost_estimate=pl.CostEstimate(flops=10**6, bytes_accessed=12 * 10**6, transcendentals=0),
        name="split_sum",
    )(*heres, *(a for pair in groups for a in pair))
    return out[: counts[0]], out[counts[0] :]


def join_kernel(pieces, out_matrix, here_ref, *refs):
    in_refs, out_refs, table = refs[:pieces], refs[pieces:-1], refs[-1]
    count = len(out_refs)
    chunk = out_refs[0].shape[3]

    def totals():
        for s in range(in_refs[0].shape[1]):
            total = in_refs[0][0, s].astype(F32)
            for ref in in_refs[1:]:
                total = total + ref[0, s].astype(F32)
            yield s, total

    @pl.when(pl.program_id(0) != out_matrix)
    def _():
        for s, total in totals():
            lanes = total.shape[1]
            total = total.reshape(2, count, 2, chunk, lanes)
            for n in range(count):
                table[n, :, :, :, s * lanes : (s + 1) * lanes] = total[:, n]

    if out_matrix >= 0:

        @pl.when(pl.program_id(0) == out_matrix)
        def _():
            for s, total in totals():
                lanes = total.shape[1]
                total = total.reshape(4, 2, 2, chunk, lanes)
                for q in range(4):
                    for y in range(2):
                        table[s % 2 * 2 + y, s // 2, :, :, q * lanes : (q + 1) * lanes] = total[q, y]

    for step, ref in enumerate(out_refs):
        ref[:, :, 0] = table[(here_ref[0] + step) % count].astype(BF16)


def join_sum(here, parts, count, out_matrix, chunk):
    mats, steps, piece, lanes = parts[0].shape
    width = steps * lanes
    return pl.pallas_call(
        functools.partial(join_kernel, len(parts), out_matrix),
        grid=(mats,),
        in_specs=[pl.BlockSpec(memory_space=pltpu.SMEM)]
        + [pl.BlockSpec((1, steps, piece, lanes), lambda m: (m, 0, 0, 0)) for _ in parts],
        out_specs=[pl.BlockSpec((2, 2, 1, chunk, width), lambda m: (0, 0, m, 0, 0)) for _ in range(count)],
        out_shape=tuple(jax.ShapeDtypeStruct((2, 2, mats, chunk, width), BF16) for _ in range(count)),
        scratch_shapes=[pltpu.VMEM((count, 2, 2, chunk, width), F32)],
        compiler_params=params(60),
        cost_estimate=pl.CostEstimate(flops=10**6, bytes_accessed=6 * 10**6, transcendentals=0),
        name="join_sum",
    )(here, *parts)


def finish_kernel(own_ref, up_ref, down_ref, left_ref, right_ref, normed_ref, inverse_ref, gain_ref, grad_ref, slots_ref, blend_ref, state_grad_ref, slot_ref):
    total = own_ref[...]
    for ref in (up_ref, down_ref, left_ref, right_ref):
        total = total + ref[...].astype(F32)
    grad = total * gain_ref[...].astype(F32)
    normed = normed_ref[...]
    grad = inverse_ref[:, :1] * (grad - normed * jnp.mean(grad * normed, axis=-1, keepdims=True))
    state_grad_ref[...] = (grad_ref[...].astype(F32) + grad).astype(BF16)
    top = grad.astype(BF16)
    rest = (grad - top.astype(F32)).astype(BF16)
    high, low = spread_weights(slots_ref, blend_ref, slot_ref.shape[0])
    slot_ref[...] = (mm(high, top, TN) + (mm(high, rest, TN) + mm(low, top, TN))).astype(BF16)


def finish(own, near, normed, inverse, gain, grad_out, slots, blend, count):
    rows, width = own.shape
    return pl.pallas_call(
        finish_kernel,
        out_shape=(
            jax.ShapeDtypeStruct((rows, width), BF16),
            jax.ShapeDtypeStruct((count, width), BF16),
        ),
        compiler_params=params(26),
        name="finish",
    )(own, *near, normed, inverse, gain, grad_out, slots, blend)


def after(value, others):
    return lax.optimization_barrier((value, others))[0]


def shifted(block, axis, step):
    count = lax.axis_size(axis)
    return lax.ppermute(block, axis, [(i, (i + step) % count) for i in range(count)])


def swapped(chunks, axis):
    return [chunks[0]] + [shifted(chunk, axis, step) for step, chunk in enumerate(chunks) if step]


def passed_along(block, axis, distance):
    count = lax.axis_size(axis)
    route = [(i, i + distance) for i in range(count) if 0 <= i + distance < count]
    return lax.ppermute(block, axis, route)


TY = ("x_hi", "y")
TX = ("z", "x_lo", "core")
X = ("x_hi", "x_lo")


def body(
    region_state,
    global_latent,
    send_rows,
    recv_slots,
    regrid_weight,
    window_mask,
    norm_gain,
    w_query,
    w_key,
    w_value,
    w_out,
    out_grad,
):
    state, grad_out = region_state[0, 0], out_grad[0, 0]
    rows, width = state.shape
    gain = norm_gain[None]
    devices = lax.axis_size(TY + TX)
    outgoing = pick_rows(send_rows, global_latent)
    incoming = lax.all_to_all(outgoing, TY + TX, split_axis=0, concat_axis=0, tiled=True)
    slot_ids, blend = recv_slots.reshape(rows, -1), regrid_weight[0, 0]
    normed_in, normed, inverse = blend_norm(slot_ids, blend, incoming, state, gain)
    tiles = (
        normed_in,
        passed_along(normed_in, TY, 1),
        passed_along(normed_in, TY, -1),
        passed_along(normed_in, TX, 1),
        passed_along(normed_in, TX, -1),
    )
    projected = project(normed_in, grad_out, w_query, w_key, w_value, w_out)
    projected += sides(tiles[3], tiles[4], w_key, w_value)
    here = {axis: lax.axis_index(axis).reshape(1) for axis in ("z", "y", "core", "x_hi", "x_lo")}
    chunk = width // devices
    ys, zs = lax.axis_size("y"), lax.axis_size("z")
    keep_y, send_y, keep_z, send_z, attended, *near, own = attend(
        here["core"], window_mask[0], tiles, grad_out, projected, w_query, w_key, w_value, ys, zs
    )
    came_y, came_z = shifted(send_y, "core", 1), shifted(send_z, "core", 1)
    returned = (
        passed_along(near[0], TY, -1),
        passed_along(near[1], TY, 1),
        passed_along(near[2], TX, -1),
        passed_along(near[3], TX, 1),
    )
    chunks_y, chunks_z = split_sum((here["y"], here["z"]), ((keep_y, came_y), (keep_z, came_z)))
    along_y, along_z = swapped(chunks_y, "y"), swapped(chunks_z, "z")
    own = after(own, (along_z[0], along_y[0]))
    state_grad, slots = finish(own, returned, normed, inverse, gain, grad_out, slot_ids, blend, incoming.shape[0])
    term = jnp.dot(after(attended, slots), w_out, preferred_element_type=F32)
    updated = (state.astype(F32) + term).astype(BF16)
    here_y, here_z = after((here["y"], here["z"]), slots)
    second_y = swapped(join_sum(here_y, along_z, ys, 1, chunk), "y")
    sent = after(slots, (along_y, updated, second_y[1]))
    sent_back = lax.all_to_all(sent, TY + TX, split_axis=0, concat_axis=0, tiled=True)
    global_grad = add_rows(send_rows, sent_back, global_latent.shape[0])
    second_z = swapped(join_sum(here_z, along_y, zs, -1, chunk), "z")
    total = jnp.concatenate([sum(piece.astype(F32) for piece in group) for group in (second_z, second_y)], axis=2)
    total = total.astype(BF16).reshape(-1, 4, chunk, width)
    place = lax.axis_index(X)
    along_x = swapped([lax.dynamic_index_in_dim(total, (place + k) % total.shape[0], 0, keepdims=False) for k in range(total.shape[0])], X)
    weight_grads = sum(piece.astype(F32) for piece in after(along_x[:1], global_grad) + along_x[1:])
    return (updated[None, None], state_grad[None, None], global_grad, weight_grads)


def solution(mesh):
    ty, tx = mesh.devices.shape
    y, z = max(ty // 2, 1), tx // 4
    fine = jax.sharding.Mesh(mesh.devices.reshape(ty // y, y, z, 2, 2), TY + TX)
    tiles = P(TY, TX)
    flat = P(TY + TX)
    return jax.shard_map(
        body,
        mesh=fine,
        in_specs=(tiles, flat, flat, tiles, tiles, tiles, P(), P(), P(), P(), P(), tiles),
        out_specs=(tiles, tiles, flat, P(None, TY + TX)),
        check_vma=False,
    )
```

```python
import functools
import jax
import jax.numpy as jnp
from jax import lax
from jax.experimental import pallas as pl
from jax.experimental.pallas import tpu as pltpu
from jax.sharding import PartitionSpec as P

HEADS = 8
HEAD_SIZE = 128
EPSILON = 1e-05
LOG2_E = 1.4426950408889634
BF16 = jnp.bfloat16
F32 = jnp.float32
NN = (((1,), (0,)), ((), ()))
NT = (((1,), (1,)), ((), ()))
TN = (((0,), (0,)), ((), ()))


def mm(left, right, dims=NN):
    return lax.dot_general(left, right, dims, preferred_element_type=F32)


def params(mib):
    return pltpu.CompilerParams(vmem_limit_bytes=mib * 1024 * 1024)


def pick_kernel(rows_ref, table_ref, out_ref):
    table_rows = table_ref.shape[0]
    hit = lax.broadcasted_iota(jnp.int32, (table_rows, rows_ref.shape[1]), 0) == rows_ref[...]
    out_ref[...] = mm(hit.astype(F32).astype(BF16), table_ref[...], TN).astype(BF16)


def pick_rows(rows, table):
    count, width, step = rows.shape[1], table.shape[1], 512
    return pl.pallas_call(
        pick_kernel,
        grid=(count // step,),
        in_specs=[
            pl.BlockSpec((1, step), lambda i: (0, i)),
            pl.BlockSpec(table.shape, lambda i: (0, 0)),
        ],
        out_specs=pl.BlockSpec((step, width), lambda i: (i, 0)),
        out_shape=jax.ShapeDtypeStruct((count, width), BF16),
        compiler_params=params(60),
        name="pick_rows",
    )(rows, table)


def add_kernel(rows_ref, sent_ref, out_ref):
    step = out_ref.shape[0]
    ids = lax.broadcasted_iota(jnp.int32, (step, rows_ref.shape[1]), 0) + pl.program_id(0) * step
    hit = (ids == rows_ref[...]).astype(F32).astype(BF16)
    out_ref[...] = mm(hit, sent_ref[...]).astype(BF16)


def add_rows(rows, sent, table_rows):
    step = 256
    return pl.pallas_call(
        add_kernel,
        grid=(table_rows // step,),
        in_specs=[
            pl.BlockSpec(rows.shape, lambda i: (0, 0)),
            pl.BlockSpec(sent.shape, lambda i: (0, 0)),
        ],
        out_specs=pl.BlockSpec((step, sent.shape[1]), lambda i: (i, 0)),
        out_shape=jax.ShapeDtypeStruct((table_rows, sent.shape[1]), BF16),
        compiler_params=params(14),
        name="add_rows",
    )(rows, sent)


def spread_weights(slots_ref, blend_ref, count):
    rows = blend_ref.shape[0]
    lanes = lax.broadcasted_iota(jnp.int32, (rows, count), 1)
    spread = jnp.zeros((rows, count), F32)
    for k in range(blend_ref.shape[1]):
        spread = spread + jnp.where(lanes == slots_ref[:, k : k + 1], blend_ref[:, k : k + 1], 0.0)
    high = spread.astype(BF16)
    return high, (spread - high.astype(F32)).astype(BF16)


def blend_kernel(slots_ref, blend_ref, incoming_ref, state_ref, gain_ref, in_ref, normed_ref, inverse_ref):
    high, low = spread_weights(slots_ref, blend_ref, incoming_ref.shape[0])
    incoming = incoming_ref[...]
    pre = state_ref[...].astype(F32) + (mm(high, incoming) + mm(low, incoming))
    inverse = lax.rsqrt(jnp.mean(pre * pre, axis=-1, keepdims=True) + EPSILON)
    normed = pre * inverse
    normed_ref[...] = normed
    inverse_ref[...] = jnp.broadcast_to(inverse, inverse_ref.shape)
    in_ref[...] = (normed * gain_ref[...].astype(F32)).astype(BF16)


def blend_norm(slots, blend, incoming, state, gain):
    rows, width = state.shape
    return pl.pallas_call(
        blend_kernel,
        out_shape=(
            jax.ShapeDtypeStruct((rows, width), BF16),
            jax.ShapeDtypeStruct((rows, width), F32),
            jax.ShapeDtypeStruct((rows, 128), F32),
        ),
        compiler_params=params(30),
        name="blend_norm",
    )(slots, blend, incoming, state, gain)


def project_kernel(in_ref, grad_ref, wq_ref, wk_ref, wv_ref, wo_ref, query_ref, key_ref, value_ref, g_ref):
    normed_in = in_ref[...]
    query_ref[...] = mm(normed_in, wq_ref[...]).astype(BF16)
    key_ref[...] = mm(normed_in, wk_ref[...]).astype(BF16)
    value_ref[...] = mm(normed_in, wv_ref[...]).astype(BF16)
    g_ref[...] = mm(grad_ref[...], wo_ref[...], NT).astype(BF16)


def project(normed_in, grad_out, w_query, w_key, w_value, w_out):
    rows, width = normed_in.shape
    lanes = 2 * HEAD_SIZE
    whole = lambda: pl.BlockSpec((rows, width), lambda h: (0, 0), pipeline_mode=pl.Buffered(1))
    columns = lambda n: pl.BlockSpec((n, lanes), lambda h: (0, h))
    return pl.pallas_call(
        project_kernel,
        grid=(width // lanes,),
        in_specs=[whole(), whole()] + [columns(width)] * 3 + [pl.BlockSpec((lanes, width), lambda h: (h, 0))],
        out_specs=[columns(rows)] * 4,
        out_shape=(jax.ShapeDtypeStruct((rows, width), BF16),) * 4,
        compiler_params=params(60),
        cost_estimate=pl.CostEstimate(flops=21 * 10**8, bytes_accessed=11 * 10**6, transcendentals=0),
        name="project",
    )(normed_in, grad_out, w_query, w_key, w_value, w_out)


def sides_kernel(left_ref, right_ref, wk_ref, wv_ref, key_ref, value_ref):
    rows = left_ref.shape[0]
    for at, ref in ((0, left_ref), (rows, right_ref)):
        key_ref[at : at + rows] = mm(ref[...], wk_ref[...]).astype(BF16)
        value_ref[at : at + rows] = mm(ref[...], wv_ref[...]).astype(BF16)


def sides(left, right, w_key, w_value):
    rows, width = left.shape
    lanes = 2 * HEAD_SIZE
    whole = lambda: pl.BlockSpec((rows, width), lambda h: (0, 0), pipeline_mode=pl.Buffered(1))
    columns = lambda n: pl.BlockSpec((n, lanes), lambda h: (0, h))
    return pl.pallas_call(
        sides_kernel,
        grid=(width // lanes,),
        in_specs=[whole(), whole(), columns(width), columns(width)],
        out_specs=[columns(2 * rows)] * 2,
        out_shape=(jax.ShapeDtypeStruct((2 * rows, width), BF16),) * 2,
        compiler_params=params(60),
        cost_estimate=pl.CostEstimate(flops=21 * 10**8, bytes_accessed=8 * 10**6, transcendentals=0),
        name="sides",
    )(left, right, w_key, w_value)


def attend_kernel(
    core_ref, mask_ref, own_ref, left_ref, right_ref, up_ref, down_ref, grad_ref,
    query_ref, own_key_ref, own_value_ref, g_ref, side_key_ref, side_value_ref, wq_ref, wk_ref, wv_ref,
    keep_y, send_y, keep_z, send_z, attended_ref, up_grad, down_grad, left_grad, right_grad, own_grad, x_all, x_turned, grads,
):
    step = pl.program_id(0)
    rows = own_ref.shape[0]
    blocks = x_all.shape[0] // rows
    ys, _, _, _, lanes = keep_y.shape
    zs, _, _, piece, _ = keep_z.shape

    @pl.when(step == 0)
    def _():
        for b, ref in enumerate((own_ref, up_ref, down_ref, left_ref, right_ref)):
            x_all[b * rows : (b + 1) * rows] = ref[...]
            x_turned[:, b * rows : (b + 1) * rows] = ref[...].T
        grads[...] = jnp.zeros_like(grads)

    grad_out = grad_ref[...]
    width = grad_out.shape[1]
    scale = HEAD_SIZE ** (-0.5)
    query, g = query_ref[...], g_ref[...]
    near = x_all[rows : 3 * rows]
    key = jnp.concatenate([own_key_ref[...], mm(near, wk_ref[...]).astype(BF16), side_key_ref[...]], axis=0)
    value = jnp.concatenate([own_value_ref[...], mm(near, wv_ref[...]).astype(BF16), side_value_ref[...]], axis=0)
    query_t, g_t = query.T, g.T
    attended_t, dquery_t, dkey, dvalue = [], [], [], []
    for h in range(lanes // HEAD_SIZE):
        at = slice(h * HEAD_SIZE, (h + 1) * HEAD_SIZE)
        raw = mm(key[:, at], query_t[at])
        scores = jnp.concatenate(
            [
                raw[b * rows : (b + 1) * rows] * (scale * LOG2_E) + jnp.where(mask_ref[0, b] > 0, 0.0, -1e30)
                for b in range(blocks)
            ],
            axis=0,
        )
        highest = jnp.max(scores, axis=0, keepdims=True)
        raised = jnp.exp2(scores - highest)
        prob = raised * (1.0 / jnp.sum(raised, axis=0, keepdims=True))
        weights = prob.astype(BF16)
        att = mm(value[:, at], weights, TN).astype(BF16)
        delta = jnp.sum(g_t[at].astype(F32) * att.astype(F32), axis=0, keepdims=True)
        dscore = (prob * (mm(value[:, at], g_t[at]) - delta) * scale).astype(BF16)
        attended_t.append(att)
        dquery_t.append(mm(key[:, at], dscore, TN).astype(BF16))
        dkey.append(mm(dscore, query[:, at]).astype(BF16))
        dvalue.append(mm(weights, g[:, at]).astype(BF16))
    attended_t = jnp.concatenate(attended_t, axis=0)
    dquery = jnp.concatenate(dquery_t, axis=0).T
    dkey = jnp.concatenate(dkey, axis=1)
    dvalue = jnp.concatenate(dvalue, axis=1)
    attended_ref[...] = attended_t.T
    grads[...] += mm(jnp.concatenate([dkey, dvalue], axis=1), jnp.concatenate([wk_ref[...], wv_ref[...]], axis=1), NT)
    grads[:rows] += mm(dquery, wq_ref[...], NT)
    first = core_ref[0] == 0

    def place(keep_ref, send_ref, at, m, where, halves):
        low, high = (half.reshape(-1, lanes) for half in halves)
        keep_ref[at, m, 0, where] = jnp.where(first, low, high).astype(BF16)
        send_ref[at, m, 0, where] = jnp.where(first, high, low).astype(BF16)

    chunk = piece // 16
    every = slice(None)
    for m, part in enumerate((mm(x_turned[:, :rows], dquery), mm(x_turned[...], dkey))):
        part = part.reshape(2, ys, zs, 2, 2, chunk, lanes)
        for y in range(ys):
            place(keep_y, send_y, y, m, every, [part[:, y, :, :, c] for c in range(2)])
    part = mm(x_turned[...], dvalue).reshape(2 * ys, zs, 2, 2, chunk, lanes)
    for z in range(zs):
        place(keep_z, send_z, z, 0, every, [part[:, z, :, c] for c in range(2)])
    part = mm(attended_t, grad_out).reshape(2, zs, 2, 2, chunk, width)
    for z in range(zs):
        for q in range(4):
            columns = slice(q * lanes, (q + 1) * lanes)
            rows_of = slice(q * piece // 4, (q + 1) * piece // 4)
            place(keep_z, send_z, z, 1, rows_of, [part[:, z, :, c, :, columns] for c in range(2)])

    @pl.when(step == pl.num_programs(0) - 1)
    def _():
        own_grad[...] = grads[:rows]
        for b, ref in enumerate((up_grad, down_grad, left_grad, right_grad), 1):
            ref[...] = grads[b * rows : (b + 1) * rows].astype(BF16)


def attend(core, mask, tiles, grad_out, projected, w_query, w_key, w_value, ys, zs):
    rows, width = grad_out.shape
    near, lanes = len(tiles), 2 * HEAD_SIZE
    own, up, down, left, right = tiles
    steps = width // lanes
    whole = lambda: pl.BlockSpec((rows, width), lambda h: (0, 0), pipeline_mode=pl.Buffered(1))
    columns = lambda: pl.BlockSpec((width, lanes), lambda h: (0, h))
    flags = lambda: pl.BlockSpec(memory_space=pltpu.SMEM)
    parts = lambda n: pl.BlockSpec((n, 2, 1, width // 2 // n, lanes), lambda h: (0, 0, h, 0, 0))
    out = lambda n: pl.BlockSpec((n, lanes), lambda h: (0, h))
    part = lambda n: jax.ShapeDtypeStruct((n, 2, steps, width // 2 // n, lanes), BF16)
    small = jax.ShapeDtypeStruct((rows, width), BF16)
    return pl.pallas_call(
        attend_kernel,
        grid=(steps,),
        in_specs=[flags(), flags()]
        + [whole() for _ in range(near + 1)]
        + [out(rows)] * 4
        + [out(2 * rows)] * 2
        + [columns()] * 3,
        out_specs=[parts(ys), parts(ys), parts(zs), parts(zs), out(rows)]
        + [whole() for _ in range(near)],
        out_shape=(part(ys), part(ys), part(zs), part(zs)) + (small,) * near + (jax.ShapeDtypeStruct((rows, width), F32),),
        scratch_shapes=[
            pltpu.VMEM((near * rows, width), BF16),
            pltpu.VMEM((width, near * rows), BF16),
            pltpu.VMEM((near * rows, width), F32),
        ],
        compiler_params=params(60),
        cost_estimate=pl.CostEstimate(flops=34 * 10**9, bytes_accessed=32 * 10**6, transcendentals=10**6),
        name="attend",
    )(core, mask, own, left, right, up, down, grad_out, *projected, w_query, w_key, w_value)


def split_kernel(counts, *refs):
    heres, refs = refs[: len(counts)], refs[len(counts) :]
    in_refs, out_refs = refs[: 2 * len(counts)], list(refs[2 * len(counts) :])
    for group, count in enumerate(counts):
        keep_ref, came_ref = in_refs[2 * group : 2 * group + 2]
        for step in range(count):
            at = (heres[group][0] + step) % count
            out_refs.pop(0)[...] = (keep_ref[at].astype(F32) + came_ref[at].astype(F32)).astype(BF16)


def split_sum(heres, groups):
    counts = tuple(keep.shape[0] for keep, _ in groups)
    steps = groups[0][0].shape[2]
    block = lambda a: pl.BlockSpec((*a.shape[:2], 1, *a.shape[3:]), lambda s: (0, 0, s, 0, 0))
    chunks = [keep.shape[1:] for keep, _ in groups for _ in range(keep.shape[0])]
    out = pl.pallas_call(
        functools.partial(split_kernel, counts),
        grid=(steps,),
        in_specs=[pl.BlockSpec(memory_space=pltpu.SMEM) for _ in heres] + [block(a) for pair in groups for a in pair],
        out_specs=[pl.BlockSpec((c[0], 1, *c[2:]), lambda s: (0, s, 0, 0)) for c in chunks],
        out_shape=tuple(jax.ShapeDtypeStruct(c, BF16) for c in chunks),
        compiler_params=params(60),
        cost_estimate=pl.CostEstimate(flops=10**6, bytes_accessed=12 * 10**6, transcendentals=0),
        name="split_sum",
    )(*heres, *(a for pair in groups for a in pair))
    return out[: counts[0]], out[counts[0] :]


def join_kernel(pieces, out_matrix, here_ref, *refs):
    in_refs, out_refs, table = refs[:pieces], refs[pieces:-1], refs[-1]
    count = len(out_refs)
    chunk = out_refs[0].shape[3]

    def totals():
        for s in range(in_refs[0].shape[1]):
            total = in_refs[0][0, s].astype(F32)
            for ref in in_refs[1:]:
                total = total + ref[0, s].astype(F32)
            yield s, total

    @pl.when(pl.program_id(0) != out_matrix)
    def _():
        for s, total in totals():
            lanes = total.shape[1]
            total = total.reshape(2, count, 2, chunk, lanes)
            for n in range(count):
                table[n, :, :, :, s * lanes : (s + 1) * lanes] = total[:, n]

    if out_matrix >= 0:

        @pl.when(pl.program_id(0) == out_matrix)
        def _():
            for s, total in totals():
                lanes = total.shape[1]
                total = total.reshape(4, 2, 2, chunk, lanes)
                for q in range(4):
                    for y in range(2):
                        table[s % 2 * 2 + y, s // 2, :, :, q * lanes : (q + 1) * lanes] = total[q, y]

    for step, ref in enumerate(out_refs):
        ref[:, :, 0] = table[(here_ref[0] + step) % count].astype(BF16)


def join_sum(here, parts, count, out_matrix, chunk):
    mats, steps, piece, lanes = parts[0].shape
    width = steps * lanes
    return pl.pallas_call(
        functools.partial(join_kernel, len(parts), out_matrix),
        grid=(mats,),
        in_specs=[pl.BlockSpec(memory_space=pltpu.SMEM)]
        + [pl.BlockSpec((1, steps, piece, lanes), lambda m: (m, 0, 0, 0)) for _ in parts],
        out_specs=[pl.BlockSpec((2, 2, 1, chunk, width), lambda m: (0, 0, m, 0, 0)) for _ in range(count)],
        out_shape=tuple(jax.ShapeDtypeStruct((2, 2, mats, chunk, width), BF16) for _ in range(count)),
        scratch_shapes=[pltpu.VMEM((count, 2, 2, chunk, width), F32)],
        compiler_params=params(60),
        cost_estimate=pl.CostEstimate(flops=10**6, bytes_accessed=6 * 10**6, transcendentals=0),
        name="join_sum",
    )(here, *parts)


def finish_kernel(own_ref, up_ref, down_ref, left_ref, right_ref, normed_ref, inverse_ref, gain_ref, grad_ref, slots_ref, blend_ref, state_grad_ref, slot_ref):
    total = own_ref[...]
    for ref in (up_ref, down_ref, left_ref, right_ref):
        total = total + ref[...].astype(F32)
    grad = total * gain_ref[...].astype(F32)
    normed = normed_ref[...]
    grad = inverse_ref[:, :1] * (grad - normed * jnp.mean(grad * normed, axis=-1, keepdims=True))
    state_grad_ref[...] = (grad_ref[...].astype(F32) + grad).astype(BF16)
    top = grad.astype(BF16)
    rest = (grad - top.astype(F32)).astype(BF16)
    high, low = spread_weights(slots_ref, blend_ref, slot_ref.shape[0])
    slot_ref[...] = (mm(high, top, TN) + (mm(high, rest, TN) + mm(low, top, TN))).astype(BF16)


def finish(own, near, normed, inverse, gain, grad_out, slots, blend, count):
    rows, width = own.shape
    return pl.pallas_call(
        finish_kernel,
        out_shape=(
            jax.ShapeDtypeStruct((rows, width), BF16),
            jax.ShapeDtypeStruct((count, width), BF16),
        ),
        compiler_params=params(26),
        name="finish",
    )(own, *near, normed, inverse, gain, grad_out, slots, blend)


def after(value, others):
    return lax.optimization_barrier((value, others))[0]


def shifted(block, axis, step):
    count = lax.axis_size(axis)
    return lax.ppermute(block, axis, [(i, (i + step) % count) for i in range(count)])


def swapped(chunks, axis):
    return [chunks[0]] + [shifted(chunk, axis, step) for step, chunk in enumerate(chunks) if step]


def passed_along(block, axis, distance):
    count = lax.axis_size(axis)
    route = [(i, i + distance) for i in range(count) if 0 <= i + distance < count]
    return lax.ppermute(block, axis, route)


TY = ("x_hi", "y")
TX = ("z", "x_lo", "core")
X = ("x_hi", "x_lo")


def body(
    region_state,
    global_latent,
    send_rows,
    recv_slots,
    regrid_weight,
    window_mask,
    norm_gain,
    w_query,
    w_key,
    w_value,
    w_out,
    out_grad,
):
    state, grad_out = region_state[0, 0], out_grad[0, 0]
    rows, width = state.shape
    gain = norm_gain[None]
    devices = lax.axis_size(TY + TX)
    outgoing = pick_rows(send_rows, global_latent)
    incoming = lax.all_to_all(outgoing, TY + TX, split_axis=0, concat_axis=0, tiled=True)
    slot_ids, blend = recv_slots.reshape(rows, -1), regrid_weight[0, 0]
    normed_in, normed, inverse = blend_norm(slot_ids, blend, incoming, state, gain)
    tiles = (
        normed_in,
        passed_along(normed_in, TY, 1),
        passed_along(normed_in, TY, -1),
        passed_along(normed_in, TX, 1),
        passed_along(normed_in, TX, -1),
    )
    projected = project(normed_in, grad_out, w_query, w_key, w_value, w_out)
    projected += sides(tiles[3], tiles[4], w_key, w_value)
    here = {axis: lax.axis_index(axis).reshape(1) for axis in ("z", "y", "core", "x_hi", "x_lo")}
    chunk = width // devices
    ys, zs = lax.axis_size("y"), lax.axis_size("z")
    keep_y, send_y, keep_z, send_z, attended, *near, own = attend(
        here["core"], window_mask[0], tiles, grad_out, projected, w_query, w_key, w_value, ys, zs
    )
    came_y, came_z = shifted(send_y, "core", 1), shifted(send_z, "core", 1)
    returned = (
        passed_along(near[0], TY, -1),
        passed_along(near[1], TY, 1),
        passed_along(near[2], TX, -1),
        passed_along(near[3], TX, 1),
    )
    chunks_y, chunks_z = split_sum((here["y"], here["z"]), ((keep_y, came_y), (keep_z, came_z)))
    along_y, along_z = swapped(chunks_y, "y"), swapped(chunks_z, "z")
    own = after(own, (along_z[0], along_y[0]))
    state_grad, slots = finish(own, returned, normed, inverse, gain, grad_out, slot_ids, blend, incoming.shape[0])
    term = jnp.dot(after(attended, slots), w_out, preferred_element_type=F32)
    updated = (state.astype(F32) + term).astype(BF16)
    here_y, here_z = after((here["y"], here["z"]), slots)
    second_y = swapped(join_sum(here_y, along_z, ys, 1, chunk), "y")
    sent = after(slots, (along_y, second_y[1]))
    sent_back = lax.all_to_all(sent, TY + TX, split_axis=0, concat_axis=0, tiled=True)
    global_grad = add_rows(send_rows, sent_back, global_latent.shape[0])
    second_z = swapped(join_sum(here_z, along_y, zs, -1, chunk), "z")
    total = jnp.concatenate([sum(piece.astype(F32) for piece in group) for group in (second_z, second_y)], axis=2)
    total = total.astype(BF16).reshape(-1, 4, chunk, width)
    total = after(total, updated)
    place = lax.axis_index(X)
    along_x = swapped([lax.dynamic_index_in_dim(total, (place + k) % total.shape[0], 0, keepdims=False) for k in range(total.shape[0])], X)
    weight_grads = sum(piece.astype(F32) for piece in after(along_x[:1], global_grad) + along_x[1:])
    return (updated[None, None], state_grad[None, None], global_grad, weight_grads)


def solution(mesh):
    ty, tx = mesh.devices.shape
    y, z = max(ty // 2, 1), tx // 4
    fine = jax.sharding.Mesh(mesh.devices.reshape(ty // y, y, z, 2, 2), TY + TX)
    tiles = P(TY, TX)
    flat = P(TY + TX)
    return jax.shard_map(
        body,
        mesh=fine,
        in_specs=(tiles, flat, flat, tiles, tiles, tiles, P(), P(), P(), P(), P(), tiles),
        out_specs=(tiles, tiles, flat, P(None, TY + TX)),
        check_vma=False,
    )
```
